256 devices in a mesh: copy: 2 (over x_lo), dp: 128 (over x_hi, z, y, core).
Axes of the slice: x: 4 (x_hi: 2, x_lo: 2; x = x_hi * 2 + x_lo), y: 4, z: 8, core: 2. Of those that a mesh axis runs over, the one named last changes fastest.
Arguments:
- features: bfloat16 [2, 49152, 1024], P('copy', 'dp'), may hold values from -100 to 100
- labels: int32 [49152], P('dp'), may hold values from 0 to 5119
- weight: bfloat16 [2, 1024, 5120], P('copy'), may hold values from -0.1875 to 0.1875
Outputs:
- update: float32 [2, 1024, 5120], P('copy', 'dp')
- loss: float32 [2], P('copy')
The draws below stay inside these ranges and needn't reach their ends.
All inputs are finite; a program needn't handle non-finite values.
Results may differ from the reference program's by a relative error of at most 0.0018.
Values may be sent and summed in bfloat16 or wider, within the bound.
A program may use at most 192 MiB of HBM per device.

```python
import math
import jax
import jax.numpy as jnp
import numpy as np
from jax import lax

D = 1024
CLASSES = 5120
IMG_DEV = 384
IMAGES = 49152
N_DP = 128


def shared_weight(key):
    return jax.random.truncated_normal(jax.random.fold_in(key, 11), -6.0, 6.0, (2, D, CLASSES), jnp.float32) * D ** (-0.5)


def draw_weight(key, part):
    return shared_weight(key).astype(jnp.bfloat16)


def draw_features(key, part):
    key = jax.random.fold_in(key, 3)
    k_base, k_col = jax.random.split(key, 2)
    base = jax.random.truncated_normal(k_base, -6.0, 6.0, (2, IMAGES, D), jnp.float32)
    column = jnp.exp(jax.random.uniform(k_col, (2, 1, D), jnp.float32) * math.log(10.0))
    values = base * column
    return values.astype(jnp.bfloat16)


def plant(values, rng, low, high):
    shape = values.shape
    place = [jax.random.randint(jax.random.fold_in(rng, axis), (), 0, shape[axis]) for axis in range(len(shape))]
    values = values.at[tuple(place)].set(low)
    longest = shape.index(max(shape))
    place[longest] = (place[longest] + 1) % shape[longest]
    return values.at[tuple(place)].set(high)


def cumulative_ranks(number_of, slope):
    loads = [(1 << 20) // math.isqrt(rank ** slope) + 1 for rank in range(1, number_of + 1)]
    width = 1 + sum(loads) // (1 << 30)
    return np.cumsum(np.array([max(1, weight // width) for weight in loads]))


def ranked_ids(rng, dims, amount, skew):
    listing = cumulative_ranks(amount, skew)
    ticket = jax.random.randint(jax.random.fold_in(rng, 1), dims, 0, int(listing[amount - 1]))
    standing = jnp.searchsorted(jnp.asarray(listing, jnp.int32), ticket, side="right")
    return jax.random.permutation(jax.random.fold_in(rng, 2), amount)[standing].astype(jnp.int32)


def setup_inputs(seed: int = 0) -> dict:
    streams_of = jax.random.split(jax.random.key(seed), 4)
    return {
        "features": draw_features(jax.random.fold_in(streams_of[3], 71), 0),
        "labels": plant(ranked_ids(streams_of[1], (IMAGES,), CLASSES, 2), jax.random.fold_in(streams_of[1], 3), 0, CLASSES - 1).astype(jnp.int32),
        "weight": draw_weight(jax.random.fold_in(streams_of[3], 71), 0),
    }


temper = 2.0
blend = 0.5
trust = 32.0
decay = 5e-05

def reference(features, labels, weight):
    blocks = features.reshape(2, N_DP, IMG_DEV, D).transpose(1, 0, 2, 3)
    label_blocks = labels.reshape(N_DP, IMG_DEV)
    classes = jnp.arange(CLASSES, dtype=jnp.int32)

    def step(carry, xs):
        grads, losses = carry
        feats, labs = xs
        onehot = (labs[:, None] == classes[None, :]).astype(jnp.float32)
        logits_all = []
        teach_all = []
        soft_all = []
        for c in range(2):
            logits = jnp.dot(feats[c], weight[c], preferred_element_type=jnp.float32)
            soft = jax.nn.softmax(logits / temper, axis=-1)
            logits_all.append(logits)
            soft_all.append(soft)
            teach_all.append(soft.astype(jnp.bfloat16))
        new_grads = []
        new_losses = []
        for c in range(2):
            logits = logits_all[c]
            probs = jax.nn.softmax(logits, axis=-1)
            other = teach_all[1 - c].astype(jnp.float32)
            scaled = logits / temper
            hard = jax.nn.logsumexp(logits, axis=-1) - lax.optimization_barrier(jnp.sum(logits * onehot, axis=-1))
            distil = jax.nn.logsumexp(scaled, axis=-1) - lax.optimization_barrier(jnp.sum(other * scaled, axis=-1))
            part = jnp.sum((1.0 - blend) * hard + blend * temper * temper * distil)
            grad_logits = ((1.0 - blend) * (probs - onehot) + blend * temper * (soft_all[c] - other)).astype(jnp.bfloat16)
            term = jnp.dot(feats[c].T, grad_logits, preferred_element_type=jnp.float32)
            new_grads.append(grads[c] + term)
            new_losses.append(losses[c] + part)
        return ((jnp.stack(new_grads), jnp.stack(new_losses)), None)
    start = (jnp.zeros((2, D, CLASSES), jnp.float32), jnp.zeros((2,), jnp.float32))
    (grads, losses), _ = lax.scan(step, start, (blocks, label_blocks))
    grads = grads / IMAGES
    losses = losses / IMAGES
    updates = []
    for c in range(2):
        wide = weight[c].astype(jnp.float32)
        gnorm = jnp.sqrt(jnp.sum(grads[c] * grads[c]))
        wnorm = jnp.sqrt(jnp.sum(wide * wide))
        updates.append(trust * wnorm / (gnorm + decay * wnorm) * (grads[c] + decay * wide))
    return (jnp.stack(updates), losses)
```

```python
import functools

import jax
import jax.numpy as jnp
from jax import lax
from jax.experimental import pallas as pl
from jax.experimental.pallas import tpu as pltpu
from jax.sharding import PartitionSpec as P

MESH = pl.DeviceIdType.MESH
NZ, NY = 8, 4
IMG = 384
D = 1024
CLASSES = 5120
SL = CLASSES // 8
IMAGES = 49152
HALF = IMG // 2
GI = 2 * IMG
trust = 32.0
decay = 5e-05
F32, BF16 = jnp.float32, jnp.bfloat16


def fold_lanes(v):
    out = v[:, 0:128]
    for k in range(1, SL // 128):
        out = out + v[:, k * 128 : (k + 1) * 128]
    return out


def fold_rows(v):
    out = v[0:8]
    for k in range(1, v.shape[0] // 8):
        out = out + v[k * 8 : (k + 1) * 8]
    return out


def kernel(
    f_in, w_in, lab_in,
    out_ref, loss_ref,
    F, FT, WS, W16, LAB, LABC, X, G, ACC, STR, COLT, LA, LS, TB, GB,
    SCZ, SCY, SCX,
    S00, R00, S01, R01, S10, R10, S11, R11,
    loc_sem, fs, fr, ws, wr, ls, lr, ss, sr, as_, ar,
    zs, zr, ys, yr, xs, xr,
    s00s, s00r, s01s, s01r, s10s, s10r, s11s, s11r,
):
    cp = lax.axis_index("copy")
    dp = lax.axis_index("dp")
    core = lax.rem(dp, 2)
    y = lax.rem(dp // 2, NY)
    z = lax.rem(dp // (2 * NY), NZ)
    xh = dp // (2 * NY * NZ)
    oc, ox, ok = 1 - cp, 1 - xh, 1 - core

    def dev(c, h, zz, yy, k):
        return (c, ((h * NZ + zz) * NY + yy) * 2 + k)

    partner = dev(oc, xh, z, y, core)
    nonp = dev(oc, ox, z, y, core)
    sib = dev(cp, xh, z, y, ok)

    def flip(v, bit):
        return 1 - v if bit else v

    group = [(a, b, c) for a in range(2) for b in range(2) for c in range(2)][1:]

    def peer(abc):
        a, b, c = abc
        return dev(flip(cp, a), flip(xh, b), z, y, flip(core, c))

    def slot(abc):
        return abc[0] * 4 + abc[1] * 2 + abc[2]

    def ypeer(o):
        return dev(cp, xh, z, lax.rem(y + o, NY), core)

    def zpeer(o):
        return dev(cp, xh, lax.rem(z + o, NZ), y, core)

    def slice_of(c, h, k):
        return pl.ds(pl.multiple_of(((c * 2 + h) * 2 + k) * SL, 128), SL)

    my_s = slice_of(cp, xh, core)

    def block(h, k, lo, rows):
        return pl.ds(pl.multiple_of((h * 2 + k) * HALF + lo, 16), rows)

    loc = [
        pltpu.make_async_copy(
            f_in.at[pl.ds(b * HALF, HALF)], F.at[0, b, block(xh, core, 0, HALF)], loc_sem.at[b]
        )
        for b in range(2)
    ] + [
        pltpu.make_async_copy(w_in.at[:, my_s], WS.at[0], loc_sem.at[2]),
        pltpu.make_async_copy(
            w_in.at[pl.ds(pl.multiple_of((dp // 2) * 16, 16), 16), :], W16, loc_sem.at[3]
        ),
        pltpu.make_async_copy(lab_in, LAB.at[xh, core], loc_sem.at[4]),
    ]
    for c in loc:
        c.start()

    peers = [peer(g) for g in group] + [ypeer(o) for o in range(1, NY)] + [zpeer(o) for o in range(1, NZ)]
    barrier = pltpu.get_barrier_semaphore()
    for p in peers:
        pl.semaphore_signal(barrier, inc=1, device_id=p, device_id_type=MESH)
    pl.semaphore_wait(barrier, len(peers))

    sends = []

    def remote(src, dst, s, r, to):
        c = pltpu.make_async_remote_copy(
            src_ref=src, dst_ref=dst, send_sem=s, recv_sem=r, device_id=to, device_id_type=MESH
        )
        return c

    def push(src, dst, s, r, to):
        c = remote(src, dst, s, r, to)
        c.start()
        sends.append(c)

    def arrive(ref, s, r):
        remote(ref, ref, s, r, partner).wait_recv()

    def quarter(yy, h):
        return pl.ds(pl.multiple_of((yy * 2 + h) * (D // NY // 2), 64), D // NY // 2)

    push(w_in.at[quarter(y, 0), slice_of(oc, xh, core)], WS.at[1, quarter(y, 0)], ws.at[0], wr.at[0], partner)
    push(w_in.at[quarter(y, 1), slice_of(oc, ox, core)], WS.at[1, quarter(y, 1)], ws.at[1], wr.at[1], nonp)

    PART = HALF // 2
    LO, HI = 0, PART

    def fpush(b, kind, own, i, h, k, lo, rows, to, src_i=None):
        at = block(h, k, lo, rows)
        src = f_in.at[pl.ds(b * HALF + lo, rows)] if own else F.at[i if src_i is None else src_i, b, at]
        push(src, F.at[i, b, at], fs.at[b, kind], fr.at[b, kind], to)

    def fwait(b, kind, i, h, k, lo, rows=PART):
        arrive(F.at[i, b, block(h, k, lo, rows)], fs.at[b, kind], fr.at[b, kind])

    def own_to_neighbours(b):
        fpush(b, 0, True, 1, xh, core, LO, PART, partner)
        fpush(b, 2, True, 1, xh, core, HI, PART, nonp)
        fpush(b, 1, True, 1, xh, core, HI, PART, partner)
        fpush(b, 3, True, 1, xh, core, LO, PART, nonp)

    def pass_on(b):
        fwait(b, 0, 1, xh, core, LO)
        fpush(b, 5, False, 0, xh, core, LO, PART, nonp, 1)
        fwait(b, 2, 1, ox, core, HI)
        fpush(b, 6, False, 0, ox, core, HI, PART, partner, 1)
        fpush(b, 7, False, 1, xh, core, LO, PART, sib)
        fpush(b, 9, False, 1, ox, core, HI, PART, sib)

    def share_rest(b):
        fwait(b, 1, 1, xh, core, HI)
        fpush(b, 8, False, 1, xh, core, HI, PART, sib)
        fwait(b, 3, 1, ox, core, LO)
        fpush(b, 10, False, 1, ox, core, LO, PART, sib)

    def share_far(b):
        fwait(b, 5, 0, ox, core, LO)
        fpush(b, 11, False, 0, ox, core, LO, PART, sib)
        fwait(b, 6, 0, ox, core, HI)
        fpush(b, 12, False, 0, ox, core, HI, PART, sib)

    def shared_neighbours(b):
        fwait(b, 7, 1, xh, ok, LO)
        fwait(b, 9, 1, ox, ok, HI)
        fwait(b, 8, 1, xh, ok, HI)
        fwait(b, 10, 1, ox, ok, LO)

    def shared_far(b):
        fwait(b, 11, 0, ox, ok, LO)
        fwait(b, 12, 0, ox, ok, HI)

    own_to_neighbours(0)
    for b in range(2):
        fpush(b, 4, True, 0, xh, core, 0, HALF, sib)

    lab_kinds = [(0, 0, 1), (0, 1, 0), (0, 1, 1)]
    for n, g in enumerate(lab_kinds):
        push(lab_in, LAB.at[xh, core], ls.at[n], lr.at[n], peer(g))

    def logits(i, b, h):
        rows = pl.ds(pl.multiple_of(h * IMG, 128), IMG)
        X[i, b, rows, :] = jnp.dot(F[i, b, rows, :], WS[i], preferred_element_type=F32)

        def body(t, carry):
            at = pl.ds(pl.multiple_of(h * IMG + t * 128, 128), 128)
            lg = X[i, b, at, :]
            m = jnp.max(lg, axis=1, keepdims=True)
            e = jnp.exp(0.5 * (lg - m))
            s = jnp.sum(e, axis=1, keepdims=True)
            s2 = jnp.sum(e * e, axis=1, keepdims=True)
            lane = lax.broadcasted_iota(jnp.int32, (128, 128), 1)
            tile = jnp.where(lane == 0, m, jnp.where(lane == 1, s, s2))
            STR[0, b, 4 * i : 4 * i + 4, at] = tile.T[0:4]
            return carry

        lax.fori_loop(0, IMG // 128, body, 0)

    def transpose(i, b, h):
        def body(t, carry):
            at = pl.ds(pl.multiple_of(h * IMG + t * 128, 128), 128)
            v = F[i, b, at, :].T
            for hh in range(2):
                for zz in range(NZ):
                    for yy in range(NY):
                        g = (hh * NZ + zz) * NY + yy
                        to = ((zz * NY + yy) if i == 0 else (yy * NZ + zz)) * 2 + hh
                        FT[i, b, to * 16 : to * 16 + 16, at] = v[g * 16 : g * 16 + 16]
            return carry

        lax.fori_loop(0, IMG // 128, body, 0)

    def label_columns():
        for h in range(2):
            for k in range(2):
                rows = jnp.concatenate(
                    [
                        jnp.broadcast_to(LAB[h, k, 0:1, t * 128 : t * 128 + 128], (128, 128)).T
                        for t in range(IMG // 128)
                    ],
                    axis=0,
                )
                for b in range(2):
                    o = (h * 2 + k) * HALF
                    LABC[b, o : o + HALF, :] = rows[b * HALF : b * HALF + HALF]

    def send_stats(b):
        for n, g in enumerate(group):
            push(STR.at[0, b], STR.at[slot(g), b], ss.at[b, n], sr.at[b, n], peer(g))

    def wait_stats(b):
        for n, g in enumerate(group):
            arrive(STR.at[slot(g), b], ss.at[b, n], sr.at[b, n])

    base = ((cp * 2 + xh) * 2 + core) * SL

    def combine(b):
        rows = []
        for i in range(2):
            vs = []
            for a in range(2):
                for n in range(4):
                    o = 4 * (i ^ a)
                    vs.append(STR[a * 4 + n, b, o : o + 4, :])
            m = functools.reduce(jnp.maximum, [v[0:1] for v in vs])
            s = s2 = 0.0
            for v in vs:
                e = jnp.exp(0.5 * (v[0:1] - m))
                s = s + v[1:2] * e
                s2 = s2 + v[2:3] * (e * e)
            per_image = (0.5 * jnp.log(s2) + 2.0 * jnp.log(s)) * 0.125
            LS[i, :, :] = LS[i] + jnp.broadcast_to(
                functools.reduce(
                    lambda p, q: p + q, [per_image[:, k * 128 : (k + 1) * 128] for k in range(GI // 128)]
                ),
                (8, 128),
            )
            rows += [m, 1.0 / s, 1.0 / s2]
        pack = jnp.concatenate(rows + rows[:2], axis=0)
        for k in range(GI // 128):
            part = pack[:, k * 128 : (k + 1) * 128]
            part = jnp.concatenate([part, jnp.zeros((120, 128), F32)], axis=0)
            COLT[k * 128 : (k + 1) * 128, :] = part.T

    R = 32

    def finish(b):
        def body(t, carry):
            at = pl.ds(pl.multiple_of(t * R, R), R)
            c = COLT[at, :]
            cls = (lax.broadcasted_iota(jnp.int32, (R, SL), 1) + base).astype(F32)
            oh = cls == LABC[b, at, 0:1]
            x0 = X[0, b, at, :] - c[:, 0:1]
            x1 = X[1, b, at, :] - c[:, 3:4]
            e0 = jnp.exp(0.5 * x0)
            e1 = jnp.exp(0.5 * x1)
            s0 = e0 * c[:, 1:2]
            s1 = e1 * c[:, 4:5]
            q0 = s0.astype(BF16).astype(F32)
            q1 = s1.astype(BF16).astype(F32)
            p0 = e0 * e0 * c[:, 2:3]
            p1 = e1 * e1 * c[:, 5:6]
            hot = jnp.where(oh, 0.5, 0.0)
            G[0, at, :] = (0.5 * p0 - hot + (s0 - q1)).astype(BF16)
            G[1, at, :] = (0.5 * p1 - hot + (s1 - q0)).astype(BF16)
            l0 = fold_lanes((q1 + hot) * x0) - c[:, 0:1] * fold_lanes(s1 - q1)
            l1 = fold_lanes((q0 + hot) * x1) - c[:, 3:4] * fold_lanes(s0 - q0)
            LA[0, :, :] = LA[0] + fold_rows(l0)
            LA[1, :, :] = LA[1] + fold_rows(l1)
            return carry

        lax.fori_loop(0, GI // R, body, 0)

    def wgrad(i, b, start, count, rows, first):
        def body(t, carry):
            j = lax.rem(start + t, D // rows)
            at = pl.ds(pl.multiple_of(j * rows, rows), rows)
            d = jnp.dot(FT[i, b, at, :], G[i], preferred_element_type=F32)
            ACC[i, at, :] = d if first else ACC[i, at, :] + d
            return carry

        lax.fori_loop(0, count, body, 0)

    LA[...] = jnp.zeros_like(LA)
    LS[...] = jnp.zeros_like(LS)

    def wsend(kind, yy, half, o):
        push(WS.at[1, quarter(yy, half)], WS.at[1, quarter(yy, half)], ws.at[kind], wr.at[kind], ypeer(o))

    def wwait(kind, yy, half):
        arrive(WS.at[1, quarter(yy, half)], ws.at[kind], wr.at[kind])

    yd, yu, yo = lax.rem(y + NY - 1, NY), lax.rem(y + 1, NY), lax.rem(y + 2, NY)

    for c in loc:
        c.wait()
    fwait(0, 4, 0, xh, ok, 0, HALF)
    logits(0, 0, xh)
    wwait(0, y, 0)
    wsend(2, y, 0, 1)
    wwait(1, y, 1)
    wsend(4, y, 1, NY - 1)
    wsend(3, y, 1, 1)
    wsend(5, y, 0, NY - 1)
    pass_on(0)
    own_to_neighbours(1)
    transpose(0, 0, xh)
    fwait(1, 4, 0, xh, ok, 0, HALF)
    wwait(2, yd, 0)
    wsend(6, yd, 0, 1)
    wwait(4, yu, 1)
    wsend(7, yu, 1, NY - 1)
    logits(0, 1, xh)
    share_rest(0)
    transpose(0, 1, xh)
    for n, (_, bb, c) in enumerate(lab_kinds):
        arrive(LAB.at[flip(xh, bb), flip(core, c)], ls.at[n], lr.at[n])
    label_columns()
    wwait(3, yd, 1)
    wwait(5, yu, 0)
    wwait(6, yo, 0)
    wwait(7, yo, 1)
    shared_neighbours(0)
    logits(1, 0, 0)
    share_far(0)
    logits(1, 0, 1)
    shared_far(0)
    logits(0, 0, ox)
    send_stats(0)
    transpose(0, 0, ox)
    pass_on(1)
    transpose(1, 0, 0)
    transpose(1, 0, 1)
    wait_stats(0)
    combine(0)
    finish(0)
    share_rest(1)
    wgrad(0, 0, 0, 4, D // 4, True)
    wgrad(1, 0, 0, 4, D // 4, True)
    shared_neighbours(1)
    logits(1, 1, 0)
    logits(1, 1, 1)
    share_far(1)
    transpose(1, 1, 0)
    transpose(1, 1, 1)
    shared_far(1)
    logits(0, 1, ox)
    send_stats(1)
    transpose(0, 1, ox)
    wait_stats(1)
    combine(1)
    finish(1)

    def ring(n, me, H, chunk, S, RB, ssem, rsem, toward):
        steps = n // 2
        for t in range(steps):
            d = steps - t
            for way in range(2):
                j = lax.rem(me + (n - d if way == 0 else d), n)
                out = S[t]
                if t == 0:
                    out[way, :, :] = chunk(j, way * H, H).astype(out.dtype)
                else:
                    arrive(RB[t - 1].at[way], ssem.at[way, t - 1], rsem.at[way, t - 1])
                    if t == 1:
                        for half in range(2):
                            v = chunk(j, half * H, H)
                            if half == way:
                                v = v + RB[0][way].astype(F32)
                            out[way, half * H : half * H + H, :] = v.astype(out.dtype)
                    else:
                        v = chunk(j, 0, 2 * H) + RB[t - 1][way].astype(F32)
                        out[way, :, :] = v.astype(out.dtype)
                push(out.at[way], RB[t].at[way], ssem.at[way, t], rsem.at[way, t], toward[way])
            yield
        for way in range(2):
            arrive(RB[steps - 1].at[way], ssem.at[way, steps - 1], rsem.at[way, steps - 1])

    ydirs, zdirs = (ypeer(NY - 1), ypeer(1)), (zpeer(NZ - 1), zpeer(1))

    def acc_chunk(i, size):
        def chunk(j, lo, rows):
            return ACC[i, pl.ds(pl.multiple_of(j * size + lo, 16), rows), :]

        return chunk

    c0, c1 = D // NZ, D // NY
    r0 = ring(NZ, z, c0 // 2, acc_chunk(0, c0), S00, R00, s00s, s00r, zdirs)
    r1 = ring(NY, y, c1 // 2, acc_chunk(1, c1), S10, R10, s10s, s10r, ydirs)

    def own0():
        at = pl.ds(pl.multiple_of(z * c0, 16), c0)
        ACC[0, at, :] = ACC[0, at, :] + (R00[-1][0].astype(F32) + R00[-1][1].astype(F32))

    def own1():
        at = pl.ds(pl.multiple_of(y * c1, 16), c1)
        ACC[1, at, :] = ACC[1, at, :] + (R10[-1][0].astype(F32) + R10[-1][1].astype(F32))

    def sub_chunk(i, first):
        def chunk(j, lo, rows):
            return ACC[i, pl.ds(pl.multiple_of(first + j * 32 + lo, 16), rows), :]

        return chunk

    q0 = ring(NY, y, 16, sub_chunk(0, z * c0), S01, R01, s01s, s01r, ydirs)
    q1 = ring(NZ, z, 16, sub_chunk(1, y * c1), S11, R11, s11s, s11r, zdirs)

    def go(gen):
        for _ in gen:
            return

    wgrad(0, 1, z + NZ // 2, 1, c0, False)
    wgrad(1, 1, y + NY // 2, 1, c1, False)
    go(r0)
    go(r1)
    wgrad(0, 1, z + NZ // 2 + 1, NZ - 1, c0, False)
    go(r0)
    wgrad(1, 1, y + NY // 2 + 1, NY - 1, c1, False)
    go(r1)
    go(r0)
    go(r0)
    go(r1)
    own1()
    go(q1)
    go(r0)
    own0()
    go(q0)
    go(q1)
    go(q0)
    go(q1)
    go(q0)
    go(q1)
    go(q1)

    inv = 1.0 / IMAGES
    sq = []
    for i in range(2):
        at = pl.ds(pl.multiple_of(z * c0 + y * 32 if i == 0 else y * c1 + z * 32, 32), 32)
        last = (R01 if i == 0 else R11)[-1]
        v = (ACC[i, at, :] + (last[0].astype(F32) + last[1].astype(F32))) * inv
        TB[i, :, :] = v
        sq.append(fold_rows(fold_lanes(v * v)))
    for n, g in enumerate(group):
        a, b, c = g
        off = pl.ds(pl.multiple_of((flip(xh, b) * 2 + flip(core, c)) * 8, 8), 8)
        push(TB.at[a, off], GB.at[:, my_s], as_.at[n], ar.at[n], peer(g))
    GB[:, my_s] = TB[0, pl.ds(pl.multiple_of((xh * 2 + core) * 8, 8), 8), :]

    vals = []
    for i in range(2):
        wq = 0.0
        for h in range(2):
            at = pl.ds(pl.multiple_of(((h * NZ + z) * NY + y) * 16, 16), 16)
            wv = WS[i, at, :].astype(F32)
            wq = wq + fold_rows(fold_lanes(wv * wv))
        lv = LS[i] * 0.125 - LA[i]
        vals.append([jnp.sum(v, axis=0, keepdims=True) for v in (sq[i], lv, wq)])
    row = lax.broadcasted_iota(jnp.int32, (8, 128), 0)
    tile = jnp.zeros((8, 128), F32)
    for r in range(3):
        v0, v1 = vals[0][r], vals[1][r]
        tile = jnp.where(row == r, jnp.where(cp == 0, v0, v1), tile)
        tile = jnp.where(row == 3 + r, jnp.where(cp == 0, v1, v0), tile)

    SCZ[0, :, :] = tile
    for o in range(1, NZ):
        push(SCZ.at[0], SCZ.at[o], zs.at[o - 1], zr.at[o - 1], zpeer(o))
    for o in range(1, NZ):
        arrive(SCZ.at[o], zs.at[o - 1], zr.at[o - 1])
    SCY[0, :, :] = jnp.sum(SCZ[...], axis=0)
    for o in range(1, NY):
        push(SCY.at[0], SCY.at[o], ys.at[o - 1], yr.at[o - 1], ypeer(o))
    for o in range(1, NY):
        arrive(SCY.at[o], ys.at[o - 1], yr.at[o - 1])
    SCX[0, :, :] = jnp.sum(SCY[...], axis=0)
    for n, g in enumerate(group):
        push(SCX.at[0], SCX.at[slot(g)], xs.at[n], xr.at[n], peer(g))
    for n, g in enumerate(group):
        arrive(SCX.at[slot(g)], xs.at[n], xr.at[n])
    total = jnp.sum(SCX[...], axis=0)
    mine = jnp.where(cp == 0, total[0:3], total[3:6])
    mine = jnp.sum(mine, axis=1, keepdims=True)
    gnorm = jnp.sqrt(mine[0:1])
    wnorm = jnp.sqrt(mine[2:3])
    scale = trust * wnorm / (gnorm + decay * wnorm)
    loss_ref[...] = jnp.broadcast_to(mine[1:2] * inv, (8, 128))

    for n, (a, b, c) in enumerate(group):
        src = slice_of(flip(cp, a), flip(xh, b), flip(core, c))
        arrive(GB.at[:, src], as_.at[n], ar.at[n])
    w16 = W16[...].astype(F32)
    own_w = jnp.where(core == 0, w16[0:8], w16[8:16])
    out_ref[...] = scale * (GB[...] + decay * own_w)

    for c in sends:
        c.wait_send()


def on_device(features, labels, weight):
    lab = jnp.broadcast_to(labels.astype(F32)[None, :], (8, IMG))
    dma = pltpu.SemaphoreType.DMA
    vm = pltpu.VMEM
    any_ = pl.BlockSpec(memory_space=pl.ANY)
    ring_bufs = []
    ring_sems = []
    for rows, types in (
        (D // NZ, [BF16] * (NZ // 2 - 1) + [F32]),
        (32, [F32] * (NY // 2)),
        (D // NY, [BF16] * (NY // 2)),
        (32, [F32] * (NZ // 2)),
    ):
        bufs = tuple(vm((2, rows // 2 if t == 0 else rows, SL), dt) for t, dt in enumerate(types))
        ring_bufs += [bufs, bufs]
        ring_sems += [dma((2, len(types)))] * 2
    update, loss = pl.pallas_call(
        kernel,
        out_shape=(
            jax.ShapeDtypeStruct((8, CLASSES), F32),
            jax.ShapeDtypeStruct((8, 128), F32),
        ),
        in_specs=[any_, any_, any_],
        out_specs=(pl.BlockSpec(memory_space=vm), pl.BlockSpec(memory_space=vm)),
        scratch_shapes=[
            vm((2, 2, GI, D), BF16),
            vm((2, 2, D, GI), BF16),
            vm((2, D, SL), BF16),
            vm((16, CLASSES), BF16),
            vm((2, 2, 8, IMG), F32),
            vm((2, GI, 128), F32),
            vm((2, 2, GI, SL), F32),
            vm((2, GI, SL), BF16),
            vm((2, D, SL), F32),
            vm((8, 2, 8, GI), F32),
            vm((GI, 128), F32),
            vm((2, 8, 128), F32),
            vm((2, 8, 128), F32),
            vm((2, 32, SL), F32),
            vm((8, CLASSES), F32),
            vm((NZ, 8, 128), F32),
            vm((NY, 8, 128), F32),
            vm((8, 8, 128), F32),
            *ring_bufs,
            dma((5,)),
            dma((2, 13)), dma((2, 13)),
            dma((8,)), dma((8,)),
            dma((3,)), dma((3,)),
            dma((2, 7)), dma((2, 7)),
            dma((7,)), dma((7,)),
            dma((NZ - 1,)), dma((NZ - 1,)),
            dma((NY - 1,)), dma((NY - 1,)),
            dma((7,)), dma((7,)),
            *ring_sems,
        ],
        compiler_params=pltpu.CompilerParams(
            collective_id=0, has_side_effects=True, vmem_limit_bytes=56 * 2**20
        ),
    )(features[0], weight[0], lab)
    return (update[None], loss[0, :1])


def solution(mesh):
    placed = (P("copy", "dp", None), P("dp"), P("copy", None, None))
    return jax.shard_map(
        on_device,
        mesh=mesh,
        in_specs=placed,
        out_specs=(P("copy", "dp", None), P("copy")),
        check_vma=False,
    )
```

```python
import functools

import jax
import jax.numpy as jnp
import numpy as np
from jax import lax
from jax.experimental import pallas as pl
from jax.experimental.pallas import tpu as pltpu
from jax.sharding import PartitionSpec as P

MESH = pl.DeviceIdType.MESH
NZ, NY = 8, 4
IMG = 384
D = 1024
CLASSES = 5120
SL = CLASSES // 8
IMAGES = 49152
HALF = IMG // 2
GI = 2 * IMG
HALF_LOG2E = 0.5 * float(np.log2(np.e))
trust = 32.0
decay = 5e-05
F32, BF16 = jnp.float32, jnp.bfloat16
STREAMS = ((1, True, 0, 256), (1, True, 256, SL), (0, False, 0, 384), (0, True, 384, SL))


def fold_lanes(v):
    out = v[:, 0:128]
    for k in range(1, SL // 128):
        out = out + v[:, k * 128 : (k + 1) * 128]
    return out


def fold_rows(v):
    out = v[0:8]
    for k in range(1, v.shape[0] // 8):
        out = out + v[k * 8 : (k + 1) * 8]
    return out


def kernel(
    f_in, w_in, lab_in,
    out_ref, loss_ref,
    LROW, F, FT, WS, W16, LAB, LABC, X, G, ACC, STR, COLT, LA, LS, TB, GB,
    SCZ, SCY, SCX,
    bufs,
    loc_sem, fs, fr, ws, wr, ls, lr, ss, sr, as_, ar,
    zs, zr, ys, yr, xs, xr,
):
    cp = lax.axis_index("copy")
    dp = lax.axis_index("dp")
    core = lax.rem(dp, 2)
    y = lax.rem(dp // 2, NY)
    z = lax.rem(dp // (2 * NY), NZ)
    xh = dp // (2 * NY * NZ)
    oc, ox, ok = 1 - cp, 1 - xh, 1 - core

    def dev(c, h, zz, yy, k):
        return (c, ((h * NZ + zz) * NY + yy) * 2 + k)

    partner = dev(oc, xh, z, y, core)
    nonp = dev(oc, ox, z, y, core)
    sib = dev(cp, xh, z, y, ok)

    def flip(v, bit):
        return 1 - v if bit else v

    group = [(a, b, c) for a in range(2) for b in range(2) for c in range(2)][1:]

    def peer(abc):
        a, b, c = abc
        return dev(flip(cp, a), flip(xh, b), z, y, flip(core, c))

    def slot(abc):
        return abc[0] * 4 + abc[1] * 2 + abc[2]

    def ypeer(o):
        return dev(cp, xh, z, lax.rem(y + o, NY), core)

    def zpeer(o):
        return dev(cp, xh, lax.rem(z + o, NZ), y, core)

    def slice_of(c, h, k):
        return pl.ds(pl.multiple_of(((c * 2 + h) * 2 + k) * SL, 128), SL)

    my_s = slice_of(cp, xh, core)
    base = ((cp * 2 + xh) * 2 + core) * SL

    def block(h, k, lo, rows):
        return pl.ds(pl.multiple_of((h * 2 + k) * HALF + lo, 16), rows)

    loc = [
        pltpu.make_async_copy(
            f_in.at[pl.ds(b * HALF, HALF)], F.at[0, b, block(xh, core, 0, HALF)], loc_sem.at[b]
        )
        for b in range(2)
    ] + [
        pltpu.make_async_copy(w_in.at[:, my_s], WS.at[0], loc_sem.at[2]),
        pltpu.make_async_copy(
            w_in.at[pl.ds(pl.multiple_of((dp // 2) * 16, 16), 16), :], W16, loc_sem.at[3]
        ),
    ]
    for c in loc:
        c.start()
    LROW[...] = jnp.broadcast_to(lab_in[...].astype(F32), (8, IMG))
    LAB[xh, core] = LROW[...]

    peers = [peer(g) for g in group] + [ypeer(o) for o in range(1, NY)] + [zpeer(o) for o in range(1, NZ)]
    barrier = pltpu.get_barrier_semaphore()
    for p in peers:
        pl.semaphore_signal(barrier, inc=1, device_id=p, device_id_type=MESH)
    pl.semaphore_wait(barrier, len(peers))

    sends = []

    def remote(src, dst, s, r, to):
        c = pltpu.make_async_remote_copy(
            src_ref=src, dst_ref=dst, send_sem=s, recv_sem=r, device_id=to, device_id_type=MESH
        )
        return c

    def push(src, dst, s, r, to):
        c = remote(src, dst, s, r, to)
        c.start()
        sends.append(c)

    def arrive(ref, s, r):
        remote(ref, ref, s, r, partner).wait_recv()

    def quarter(yy, h):
        return pl.ds(pl.multiple_of((yy * 2 + h) * (D // NY // 2), 64), D // NY // 2)

    push(w_in.at[quarter(y, 0), slice_of(oc, xh, core)], WS.at[1, quarter(y, 0)], ws.at[0], wr.at[0], partner)
    push(w_in.at[quarter(y, 1), slice_of(oc, ox, core)], WS.at[1, quarter(y, 1)], ws.at[1], wr.at[1], nonp)

    PART = HALF // 2
    LO, HI = 0, PART

    def fpush(b, kind, own, i, h, k, lo, rows, to, src_i=None):
        at = block(h, k, lo, rows)
        src = f_in.at[pl.ds(b * HALF + lo, rows)] if own else F.at[i if src_i is None else src_i, b, at]
        push(src, F.at[i, b, at], fs.at[b, kind], fr.at[b, kind], to)

    def fwait(b, kind, i, h, k, lo, rows=PART):
        arrive(F.at[i, b, block(h, k, lo, rows)], fs.at[b, kind], fr.at[b, kind])

    def own_to_neighbours(b):
        fpush(b, 0, True, 1, xh, core, LO, PART, partner)
        fpush(b, 2, True, 1, xh, core, HI, PART, nonp)
        fpush(b, 1, True, 1, xh, core, HI, PART, partner)
        fpush(b, 3, True, 1, xh, core, LO, PART, nonp)

    def pass_on(b):
        fwait(b, 0, 1, xh, core, LO)
        fpush(b, 5, False, 0, xh, core, LO, PART, nonp, 1)
        fwait(b, 2, 1, ox, core, HI)
        fpush(b, 6, False, 0, ox, core, HI, PART, partner, 1)
        fpush(b, 7, False, 1, xh, core, LO, PART, sib)
        fpush(b, 9, False, 1, ox, core, HI, PART, sib)

    def share_rest(b):
        fwait(b, 1, 1, xh, core, HI)
        fpush(b, 8, False, 1, xh, core, HI, PART, sib)
        fwait(b, 3, 1, ox, core, LO)
        fpush(b, 10, False, 1, ox, core, LO, PART, sib)

    def share_far(b):
        fwait(b, 5, 0, ox, core, LO)
        fpush(b, 11, False, 0, ox, core, LO, PART, sib)
        fwait(b, 6, 0, ox, core, HI)
        fpush(b, 12, False, 0, ox, core, HI, PART, sib)

    def shared_neighbours(b):
        fwait(b, 7, 1, xh, ok, LO)
        fwait(b, 9, 1, ox, ok, HI)
        fwait(b, 8, 1, xh, ok, HI)
        fwait(b, 10, 1, ox, ok, LO)

    def shared_far(b):
        fwait(b, 11, 0, ox, ok, LO)
        fwait(b, 12, 0, ox, ok, HI)

    own_to_neighbours(0)
    for b in range(2):
        fpush(b, 4, True, 0, xh, core, 0, HALF, sib)

    lab_kinds = [(0, 0, 1), (0, 1, 0), (0, 1, 1)]
    for n, g in enumerate(lab_kinds):
        push(LROW, LAB.at[xh, core], ls.at[n], lr.at[n], peer(g))

    def logits(i, b, h):
        rows = pl.ds(pl.multiple_of(h * IMG, 128), IMG)
        X[i, b, rows, :] = jnp.dot(F[i, b, rows, :], WS[i], preferred_element_type=F32)

        def body(t, carry):
            at = pl.ds(pl.multiple_of(h * IMG + t * 128, 128), 128)
            lg = [X[i, b, at, k * 128 : k * 128 + 128] for k in range(SL // 128)]
            m = jnp.max(functools.reduce(jnp.maximum, lg), axis=1, keepdims=True)
            s = s2 = 0.0
            for v in lg:
                e = jnp.exp2((v - m) * HALF_LOG2E)
                s = s + e
                s2 = s2 + e * e
            s = jnp.sum(s, axis=1, keepdims=True)
            s2 = jnp.sum(s2, axis=1, keepdims=True)
            lane = lax.broadcasted_iota(jnp.int32, (128, 128), 1)
            tile = jnp.where(lane == 0, m, jnp.where(lane == 1, s, s2))
            STR[0, b, 4 * i : 4 * i + 4, at] = tile.T[0:4]
            return carry

        lax.fori_loop(0, IMG // 128, body, 0, unroll=True)

    def transpose(i, b, h):
        def body(t, carry):
            at = pl.ds(pl.multiple_of(h * IMG + t * 128, 128), 128)
            v = F[i, b, at, :].T
            for hh in range(2):
                for zz in range(NZ):
                    for yy in range(NY):
                        g = (hh * NZ + zz) * NY + yy
                        to = ((zz * NY + yy) if i == 0 else (yy * NZ + zz)) * 2 + hh
                        FT[i, b, to * 16 : to * 16 + 16, at] = v[g * 16 : g * 16 + 16]
            return carry

        lax.fori_loop(0, IMG // 128, body, 0)

    def label_columns():
        for h in range(2):
            for k in range(2):
                rows = jnp.concatenate(
                    [
                        jnp.broadcast_to(LAB[h, k, 0:1, t * 128 : t * 128 + 128], (128, 128)).T
                        for t in range(IMG // 128)
                    ],
                    axis=0,
                )
                for b in range(2):
                    o = (h * 2 + k) * HALF
                    LABC[b, o : o + HALF, :] = rows[b * HALF : b * HALF + HALF] - base.astype(F32)

    def send_stats(b):
        for n, g in enumerate(group):
            push(STR.at[0, b], STR.at[slot(g), b], ss.at[b, n], sr.at[b, n], peer(g))

    def wait_stats(b):
        for n, g in enumerate(group):
            arrive(STR.at[slot(g), b], ss.at[b, n], sr.at[b, n])

    def combine(b):
        rows = []
        for i in range(2):
            vs = []
            for a in range(2):
                for n in range(4):
                    o = 4 * (i ^ a)
                    vs.append(STR[a * 4 + n, b, o : o + 4, :])
            m = functools.reduce(jnp.maximum, [v[0:1] for v in vs])
            s = s2 = 0.0
            for v in vs:
                e = jnp.exp(0.5 * (v[0:1] - m))
                s = s + v[1:2] * e
                s2 = s2 + v[2:3] * (e * e)
            per_image = (0.5 * jnp.log(s2) + 2.0 * jnp.log(s)) * 0.125
            LS[i, :, :] = LS[i] + jnp.broadcast_to(
                functools.reduce(
                    lambda p, q: p + q, [per_image[:, k * 128 : (k + 1) * 128] for k in range(GI // 128)]
                ),
                (8, 128),
            )
            rows += [m, 1.0 / s, 0.5 / s2]
        pack = jnp.concatenate(rows + rows[:2], axis=0)
        for k in range(GI // 128):
            part = pack[:, k * 128 : (k + 1) * 128]
            part = jnp.concatenate([part, jnp.zeros((120, 128), F32)], axis=0)
            COLT[k * 128 : (k + 1) * 128, :] = part.T

    R = 32

    def finish(b):
        def body(t, carry):
            at = pl.ds(pl.multiple_of(t * R, R), R)
            c = COLT[at, :]
            m0, r0, k0, m1, r1, k1 = (jnp.broadcast_to(c[:, j : j + 1], (R, 128)) for j in range(6))
            lab = jnp.broadcast_to(LABC[b, at, 0:1], (R, 128))
            lane = lax.broadcasted_iota(jnp.int32, (R, 128), 1).astype(F32)
            l0 = l1 = d0 = d1 = 0.0
            for k in range(SL // 128):
                ln = slice(k * 128, k * 128 + 128)
                x0 = X[0, b, at, ln] - m0
                x1 = X[1, b, at, ln] - m1
                e0 = jnp.exp2(x0 * HALF_LOG2E)
                e1 = jnp.exp2(x1 * HALF_LOG2E)
                s0 = e0 * r0
                s1 = e1 * r1
                q0 = s0.astype(BF16).astype(F32)
                q1 = s1.astype(BF16).astype(F32)
                hot = jnp.where(lane == lab - float(k * 128), 0.5, 0.0)
                G[0, at, ln] = (e0 * e0 * k0 - hot + (s0 - q1)).astype(BF16)
                G[1, at, ln] = (e1 * e1 * k1 - hot + (s1 - q0)).astype(BF16)
                l0 = l0 + (q1 + hot) * x0
                l1 = l1 + (q0 + hot) * x1
                d0 = d0 + (s0 - q0)
                d1 = d1 + (s1 - q1)
            l0 = l0 - m0 * d1
            l1 = l1 - m1 * d0
            LA[0, :, :] = LA[0] + fold_rows(l0)
            LA[1, :, :] = LA[1] + fold_rows(l1)
            return carry

        lax.fori_loop(0, GI // R, body, 0)

    def wgrad(i, b, start, count, rows, first):
        def body(t, carry):
            j = lax.rem(start + t, D // rows)
            at = pl.ds(pl.multiple_of(j * rows, rows), rows)
            d = jnp.dot(FT[i, b, at, :], G[i], preferred_element_type=F32)
            ACC[i, at, :] = d if first else ACC[i, at, :] + d
            return carry

        lax.fori_loop(0, count, body, 0)

    LA[...] = jnp.zeros_like(LA)
    LS[...] = jnp.zeros_like(LS)

    def wsend(kind, yy, half, o):
        push(WS.at[1, quarter(yy, half)], WS.at[1, quarter(yy, half)], ws.at[kind], wr.at[kind], ypeer(o))

    def wwait(kind, yy, half):
        arrive(WS.at[1, quarter(yy, half)], ws.at[kind], wr.at[kind])

    yd, yu, yo = lax.rem(y + NY - 1, NY), lax.rem(y + 1, NY), lax.rem(y + 2, NY)

    for c in loc:
        c.wait()
    fwait(0, 4, 0, xh, ok, 0, HALF)
    logits(0, 0, xh)
    wwait(0, y, 0)
    wsend(2, y, 0, 1)
    wwait(1, y, 1)
    wsend(4, y, 1, NY - 1)
    wsend(3, y, 1, 1)
    wsend(5, y, 0, NY - 1)
    pass_on(0)
    own_to_neighbours(1)
    transpose(0, 0, xh)
    fwait(1, 4, 0, xh, ok, 0, HALF)
    wwait(2, yd, 0)
    wsend(6, yd, 0, 1)
    wwait(4, yu, 1)
    wsend(7, yu, 1, NY - 1)
    logits(0, 1, xh)
    share_rest(0)
    transpose(0, 1, xh)
    for n, (_, bb, c) in enumerate(lab_kinds):
        arrive(LAB.at[flip(xh, bb), flip(core, c)], ls.at[n], lr.at[n])
    label_columns()
    wwait(3, yd, 1)
    wwait(5, yu, 0)
    wwait(6, yo, 0)
    wwait(7, yo, 1)
    shared_neighbours(0)
    logits(1, 0, 0)
    share_far(0)
    logits(1, 0, 1)
    shared_far(0)
    logits(0, 0, ox)
    send_stats(0)
    transpose(0, 0, ox)
    pass_on(1)
    transpose(1, 0, 0)
    transpose(1, 0, 1)
    wait_stats(0)
    combine(0)
    finish(0)
    share_rest(1)
    wgrad(0, 0, 0, 4, D // 4, True)
    wgrad(1, 0, 0, 4, D // 4, True)
    shared_neighbours(1)
    logits(1, 1, 0)
    logits(1, 1, 1)
    share_far(1)
    transpose(1, 1, 0)
    transpose(1, 1, 1)
    shared_far(1)
    logits(0, 1, ox)
    send_stats(1)
    transpose(0, 1, ox)
    wait_stats(1)
    combine(1)
    finish(1)

    def ring(n, me, H, chunk, S, RB, ssem, rsem, toward):
        steps = n // 2
        for t in range(steps):
            d = steps - t
            for way in range(2):
                j = lax.rem(me + (n - d if way == 0 else d), n)
                out = S[t]
                if t == 0:
                    out[way, :, :] = chunk(j, way * H, H).astype(out.dtype)
                else:
                    arrive(RB[t - 1].at[way], ssem.at[way, t - 1], rsem.at[way, t - 1])
                    if t == 1:
                        for half in range(2):
                            v = chunk(j, half * H, H)
                            if half == way:
                                v = v + RB[0][way].astype(F32)
                            out[way, half * H : half * H + H, :] = v.astype(out.dtype)
                    else:
                        v = chunk(j, 0, 2 * H) + RB[t - 1][way].astype(F32)
                        out[way, :, :] = v.astype(out.dtype)
                push(out.at[way], RB[t].at[way], ssem.at[way, t], rsem.at[way, t], toward[way])
            yield
        for way in range(2):
            arrive(RB[steps - 1].at[way], ssem.at[way, steps - 1], rsem.at[way, steps - 1])

    c0, c1 = D // NZ, D // NY

    def plain(i, size, cols):
        def chunk(j, lo, rows):
            return ACC[i, pl.ds(pl.multiple_of(j * size + lo, 16), rows), cols]

        return chunk

    def strided(i, cols):
        def chunk(j, lo, rows):
            return jnp.concatenate(
                [
                    ACC[i, pl.ds(pl.multiple_of((zz * NY + j) * 32, 32), 32), cols]
                    for zz in range(lo // 32, (lo + rows) // 32)
                ],
                axis=0,
            )

        return chunk

    def of_result(ref):
        def chunk(j, lo, rows):
            return ref[pl.ds(pl.multiple_of(j * 32 + lo, 16), rows), :]

        return chunk

    inv = 1.0 / IMAGES
    sq = [0.0, 0.0]

    class Stream:
        def __init__(self, n):
            self.role, y_first, lo, hi = STREAMS[n]
            self.cols = slice(lo, hi)
            buf = bufs[n]
            self.res, (s1, r1), (s2, r2) = buf["res"], buf["first"], buf["second"]
            sems1, sems2 = buf["sems"]
            ydirs, zdirs = (ypeer(NY - 1), ypeer(1)), (zpeer(NZ - 1), zpeer(1))
            first = (NY, y, ydirs) if y_first else (NZ, z, zdirs)
            second = (NZ, z, zdirs) if y_first else (NY, y, ydirs)
            self.size, self.me1, self.me2 = D // first[0], first[1], second[1]
            if y_first and self.role == 0:
                self.chunk = strided(0, self.cols)
            else:
                self.chunk = plain(self.role, self.size, self.cols)
            self.r1, self.r2 = r1, r2
            self.a = ring(first[0], first[1], self.size // 2, self.chunk, s1, r1, *sems1, first[2])
            self.b = ring(second[0], second[1], 16, of_result(self.res), s2, r2, *sems2, second[2])

        def one(self):
            next(self.a, None)

        def turn(self):
            next(self.a, None)
            own = self.chunk(self.me1, 0, self.size)
            self.res[...] = own + (self.r1[-1][0].astype(F32) + self.r1[-1][1].astype(F32))
            next(self.b, None)

        def two(self):
            next(self.b, None)

        def end(self):
            next(self.b, None)
            at = pl.ds(pl.multiple_of(self.me2 * 32, 32), 32)
            v = (self.res[at, :] + (self.r2[-1][0].astype(F32) + self.r2[-1][1].astype(F32))) * inv
            TB[self.role, :, self.cols] = v
            q = v * v
            for k in range(v.shape[1] // 128):
                sq[self.role] = sq[self.role] + fold_rows(q[:, k * 128 : k * 128 + 128])

    A1, A2, B1, B2 = (Stream(n) for n in range(4))
    wgrad(1, 1, y + NY // 2, 1, c1, False)
    A1.one()
    A2.one()
    wgrad(0, 1, z + NZ // 2, 1, c0, False)
    B1.one()
    wgrad(1, 1, y + NY // 2 + 1, NY - 1, c1, False)
    A1.one()
    wgrad(0, 1, z + NZ // 2 + 1, NZ - 1, c0, False)
    B1.one()
    B2.one()
    A2.one()
    B1.one()
    A1.turn()
    B1.one()
    B2.one()
    A1.two()
    A2.turn()
    A1.two()
    B1.turn()
    A1.two()
    A2.two()
    B1.two()
    B2.turn()
    A1.end()
    A2.two()
    B1.end()
    B2.two()
    A2.two()
    B2.two()
    A2.end()
    B2.two()
    B2.end()

    for n, g in enumerate(group):
        a, b, c = g
        off = pl.ds(pl.multiple_of((flip(xh, b) * 2 + flip(core, c)) * 8, 8), 8)
        push(TB.at[a, off], GB.at[:, my_s], as_.at[n], ar.at[n], peer(g))
    GB[:, my_s] = TB[0, pl.ds(pl.multiple_of((xh * 2 + core) * 8, 8), 8), :]

    vals = []
    for i in range(2):
        wq = 0.0
        for h in range(2):
            at = pl.ds(pl.multiple_of(((h * NZ + z) * NY + y) * 16, 16), 16)
            wv = WS[i, at, :].astype(F32)
            wq = wq + fold_rows(fold_lanes(wv * wv))
        lv = LS[i] * 0.125 - LA[i]
        vals.append([jnp.sum(v, axis=0, keepdims=True) for v in (sq[i], lv, wq)])
    row = lax.broadcasted_iota(jnp.int32, (8, 128), 0)
    tile = jnp.zeros((8, 128), F32)
    for r in range(3):
        v0, v1 = vals[0][r], vals[1][r]
        tile = jnp.where(row == r, jnp.where(cp == 0, v0, v1), tile)
        tile = jnp.where(row == 3 + r, jnp.where(cp == 0, v1, v0), tile)

    SCZ[0, :, :] = tile
    for o in range(1, NZ):
        push(SCZ.at[0], SCZ.at[o], zs.at[o - 1], zr.at[o - 1], zpeer(o))
    for o in range(1, NZ):
        arrive(SCZ.at[o], zs.at[o - 1], zr.at[o - 1])
    SCY[0, :, :] = jnp.sum(SCZ[...], axis=0)
    for o in range(1, NY):
        push(SCY.at[0], SCY.at[o], ys.at[o - 1], yr.at[o - 1], ypeer(o))
    for o in range(1, NY):
        arrive(SCY.at[o], ys.at[o - 1], yr.at[o - 1])
    SCX[0, :, :] = jnp.sum(SCY[...], axis=0)
    for n, g in enumerate(group):
        push(SCX.at[0], SCX.at[slot(g)], xs.at[n], xr.at[n], peer(g))
    for n, g in enumerate(group):
        arrive(SCX.at[slot(g)], xs.at[n], xr.at[n])
    total = jnp.sum(SCX[...], axis=0)
    mine = jnp.where(cp == 0, total[0:3], total[3:6])
    mine = jnp.sum(mine, axis=1, keepdims=True)
    gnorm = jnp.sqrt(mine[0:1])
    wnorm = jnp.sqrt(mine[2:3])
    scale = trust * wnorm / (gnorm + decay * wnorm)
    loss_ref[0] = jnp.sum(mine[1:2]) * inv

    for n, (a, b, c) in enumerate(group):
        src = slice_of(flip(cp, a), flip(xh, b), flip(core, c))
        arrive(GB.at[:, src], as_.at[n], ar.at[n])
    w16 = W16[...].astype(F32)
    own_w = jnp.where(core == 0, w16[0:8], w16[8:16])
    out_ref[...] = scale * (GB[...] + decay * own_w)

    for c in sends:
        c.wait_send()


def on_device(features, labels, weight):
    lab = labels[None, :]
    dma = pltpu.SemaphoreType.DMA
    vm = pltpu.VMEM
    any_ = pl.BlockSpec(memory_space=pl.ANY)
    def buffers(rows, width, types):
        one = tuple(vm((2, rows // 2 if t == 0 else rows, width), dt) for t, dt in enumerate(types))
        return (one, one)

    bufs = []
    for _, y_first, lo, hi in STREAMS:
        if y_first:
            n1, n2, types = NY, NZ, [BF16] * (NY // 2)
        else:
            n1, n2, types = NZ, NY, [BF16] * (NZ // 2 - 1) + [F32]
        bufs.append(
            dict(
                res=vm((D // n1, hi - lo), F32),
                first=buffers(D // n1, hi - lo, types),
                second=buffers(32, hi - lo, [F32] * (n2 // 2)),
                sems=((dma((2, n1 // 2)), dma((2, n1 // 2))), (dma((2, n2 // 2)), dma((2, n2 // 2)))),
            )
        )
    update, loss = pl.pallas_call(
        kernel,
        out_shape=(
            jax.ShapeDtypeStruct((8, CLASSES), F32),
            jax.ShapeDtypeStruct((1,), F32),
        ),
        in_specs=[any_, any_, pl.BlockSpec(memory_space=vm)],
        out_specs=(pl.BlockSpec(memory_space=vm), pl.BlockSpec(memory_space=pltpu.SMEM)),
        scratch_shapes=[
            vm((8, IMG), F32),
            vm((2, 2, GI, D), BF16),
            vm((2, 2, D, GI), BF16),
            vm((2, D, SL), BF16),
            vm((16, CLASSES), BF16),
            vm((2, 2, 8, IMG), F32),
            vm((2, GI, 128), F32),
            vm((2, 2, GI, SL), F32),
            vm((2, GI, SL), BF16),
            vm((2, D, SL), F32),
            vm((8, 2, 8, GI), F32),
            vm((GI, 128), F32),
            vm((2, 8, 128), F32),
            vm((2, 8, 128), F32),
            vm((2, 32, SL), F32),
            vm((8, CLASSES), F32),
            vm((NZ, 8, 128), F32),
            vm((NY, 8, 128), F32),
            vm((8, 8, 128), F32),
            bufs,
            dma((4,)),
            dma((2, 13)), dma((2, 13)),
            dma((8,)), dma((8,)),
            dma((3,)), dma((3,)),
            dma((2, 7)), dma((2, 7)),
            dma((7,)), dma((7,)),
            dma((NZ - 1,)), dma((NZ - 1,)),
            dma((NY - 1,)), dma((NY - 1,)),
            dma((7,)), dma((7,)),
        ],
        compiler_params=pltpu.CompilerParams(
            collective_id=0, has_side_effects=True, vmem_limit_bytes=56 * 2**20
        ),
    )(features[0], weight[0], lab)
    return (update[None], loss)


def solution(mesh):
    placed = (P("copy", "dp", None), P("dp"), P("copy", None, None))
    return jax.shard_map(
        on_device,
        mesh=mesh,
        in_specs=placed,
        out_specs=(P("copy", "dp", None), P("copy")),
        check_vma=False,
    )
```

```python
import functools

import jax
import jax.numpy as jnp
import numpy as np
from jax import lax
from jax.experimental import pallas as pl
from jax.experimental.pallas import tpu as pltpu
from jax.sharding import PartitionSpec as P

MESH = pl.DeviceIdType.MESH
NZ, NY = 8, 4
IMG = 384
D = 1024
CLASSES = 5120
SL = CLASSES // 8
IMAGES = 49152
HALF = IMG // 2
GI = 2 * IMG
HALF_LOG2E = 0.5 * float(np.log2(np.e))
trust = 32.0
decay = 5e-05
F32, BF16 = jnp.float32, jnp.bfloat16


def fold_lanes(v):
    out = v[:, 0:128]
    for k in range(1, SL // 128):
        out = out + v[:, k * 128 : (k + 1) * 128]
    return out


def fold_rows(v):
    out = v[0:8]
    for k in range(1, v.shape[0] // 8):
        out = out + v[k * 8 : (k + 1) * 8]
    return out


def kernel(
    f_in, w_in, lab_in,
    out_ref, loss_ref,
    F, FT, WS, W16, LAB, LABC, X, G, ACC, STR, COLT, LA, LS, TB, GB,
    SCZ, SCY, SCX,
    S00, R00, S01, R01, S10, R10, S11, R11,
    loc_sem, fs, fr, ws, wr, ls, lr, ss, sr, as_, ar,
    zs, zr, ys, yr, xs, xr,
    s00s, s00r, s01s, s01r, s10s, s10r, s11s, s11r,
):
    cp = lax.axis_index("copy")
    dp = lax.axis_index("dp")
    core = lax.rem(dp, 2)
    y = lax.rem(dp // 2, NY)
    z = lax.rem(dp // (2 * NY), NZ)
    xh = dp // (2 * NY * NZ)
    oc, ox, ok = 1 - cp, 1 - xh, 1 - core

    def dev(c, h, zz, yy, k):
        return (c, ((h * NZ + zz) * NY + yy) * 2 + k)

    partner = dev(oc, xh, z, y, core)
    nonp = dev(oc, ox, z, y, core)
    sib = dev(cp, xh, z, y, ok)

    def flip(v, bit):
        return 1 - v if bit else v

    group = [(a, b, c) for a in range(2) for b in range(2) for c in range(2)][1:]

    def peer(abc):
        a, b, c = abc
        return dev(flip(cp, a), flip(xh, b), z, y, flip(core, c))

    def slot(abc):
        return abc[0] * 4 + abc[1] * 2 + abc[2]

    def ypeer(o):
        return dev(cp, xh, z, lax.rem(y + o, NY), core)

    def zpeer(o):
        return dev(cp, xh, lax.rem(z + o, NZ), y, core)

    def slice_of(c, h, k):
        return pl.ds(pl.multiple_of(((c * 2 + h) * 2 + k) * SL, 128), SL)

    my_s = slice_of(cp, xh, core)
    base = ((cp * 2 + xh) * 2 + core) * SL

    def block(h, k, lo, rows):
        return pl.ds(pl.multiple_of((h * 2 + k) * HALF + lo, 16), rows)

    loc = [
        pltpu.make_async_copy(
            f_in.at[pl.ds(b * HALF, HALF)], F.at[0, b, block(xh, core, 0, HALF)], loc_sem.at[b]
        )
        for b in range(2)
    ] + [
        pltpu.make_async_copy(w_in.at[:, my_s], WS.at[0], loc_sem.at[2]),
        pltpu.make_async_copy(
            w_in.at[pl.ds(pl.multiple_of((dp // 2) * 16, 16), 16), :], W16, loc_sem.at[3]
        ),
        pltpu.make_async_copy(lab_in, LAB.at[xh, core], loc_sem.at[4]),
    ]
    for c in loc:
        c.start()

    peers = [peer(g) for g in group] + [ypeer(o) for o in range(1, NY)] + [zpeer(o) for o in range(1, NZ)]
    barrier = pltpu.get_barrier_semaphore()
    for p in peers:
        pl.semaphore_signal(barrier, inc=1, device_id=p, device_id_type=MESH)
    pl.semaphore_wait(barrier, len(peers))

    sends = []

    def remote(src, dst, s, r, to):
        c = pltpu.make_async_remote_copy(
            src_ref=src, dst_ref=dst, send_sem=s, recv_sem=r, device_id=to, device_id_type=MESH
        )
        return c

    def push(src, dst, s, r, to):
        c = remote(src, dst, s, r, to)
        c.start()
        sends.append(c)

    def arrive(ref, s, r):
        remote(ref, ref, s, r, partner).wait_recv()

    def quarter(yy, h):
        return pl.ds(pl.multiple_of((yy * 2 + h) * (D // NY // 2), 64), D // NY // 2)

    push(w_in.at[quarter(y, 0), slice_of(oc, xh, core)], WS.at[1, quarter(y, 0)], ws.at[0], wr.at[0], partner)
    push(w_in.at[quarter(y, 1), slice_of(oc, ox, core)], WS.at[1, quarter(y, 1)], ws.at[1], wr.at[1], nonp)

    PART = HALF // 2
    LO, HI = 0, PART

    def fpush(b, kind, own, i, h, k, lo, rows, to, src_i=None):
        at = block(h, k, lo, rows)
        src = f_in.at[pl.ds(b * HALF + lo, rows)] if own else F.at[i if src_i is None else src_i, b, at]
        push(src, F.at[i, b, at], fs.at[b, kind], fr.at[b, kind], to)

    def fwait(b, kind, i, h, k, lo, rows=PART):
        arrive(F.at[i, b, block(h, k, lo, rows)], fs.at[b, kind], fr.at[b, kind])

    def own_to_neighbours(b):
        fpush(b, 0, True, 1, xh, core, LO, PART, partner)
        fpush(b, 2, True, 1, xh, core, HI, PART, nonp)
        fpush(b, 1, True, 1, xh, core, HI, PART, partner)
        fpush(b, 3, True, 1, xh, core, LO, PART, nonp)

    def pass_on(b):
        fwait(b, 0, 1, xh, core, LO)
        fpush(b, 5, False, 0, xh, core, LO, PART, nonp, 1)
        fwait(b, 2, 1, ox, core, HI)
        fpush(b, 6, False, 0, ox, core, HI, PART, partner, 1)
        fpush(b, 7, False, 1, xh, core, LO, PART, sib)
        fpush(b, 9, False, 1, ox, core, HI, PART, sib)

    def share_rest(b):
        fwait(b, 1, 1, xh, core, HI)
        fpush(b, 8, False, 1, xh, core, HI, PART, sib)
        fwait(b, 3, 1, ox, core, LO)
        fpush(b, 10, False, 1, ox, core, LO, PART, sib)

    def share_far(b):
        fwait(b, 5, 0, ox, core, LO)
        fpush(b, 11, False, 0, ox, core, LO, PART, sib)
        fwait(b, 6, 0, ox, core, HI)
        fpush(b, 12, False, 0, ox, core, HI, PART, sib)

    def shared_neighbours(b):
        fwait(b, 7, 1, xh, ok, LO)
        fwait(b, 9, 1, ox, ok, HI)
        fwait(b, 8, 1, xh, ok, HI)
        fwait(b, 10, 1, ox, ok, LO)

    def shared_far(b):
        fwait(b, 11, 0, ox, ok, LO)
        fwait(b, 12, 0, ox, ok, HI)

    own_to_neighbours(0)
    for b in range(2):
        fpush(b, 4, True, 0, xh, core, 0, HALF, sib)

    lab_kinds = [(0, 0, 1), (0, 1, 0), (0, 1, 1)]
    for n, g in enumerate(lab_kinds):
        push(lab_in, LAB.at[xh, core], ls.at[n], lr.at[n], peer(g))

    def logits(i, b, h):
        rows = pl.ds(pl.multiple_of(h * IMG, 128), IMG)
        X[i, b, rows, :] = jnp.dot(F[i, b, rows, :], WS[i], preferred_element_type=F32)

        def body(t, carry):
            at = pl.ds(pl.multiple_of(h * IMG + t * 128, 128), 128)
            lg = [X[i, b, at, k * 128 : k * 128 + 128] for k in range(SL // 128)]
            m = jnp.max(functools.reduce(jnp.maximum, lg), axis=1, keepdims=True)
            s = s2 = 0.0
            for v in lg:
                e = jnp.exp2((v - m) * HALF_LOG2E)
                s = s + e
                s2 = s2 + e * e
            s = jnp.sum(s, axis=1, keepdims=True)
            s2 = jnp.sum(s2, axis=1, keepdims=True)
            lane = lax.broadcasted_iota(jnp.int32, (128, 128), 1)
            tile = jnp.where(lane == 0, m, jnp.where(lane == 1, s, s2))
            STR[0, b, 4 * i : 4 * i + 4, at] = tile.T[0:4]
            return carry

        lax.fori_loop(0, IMG // 128, body, 0, unroll=True)

    def transpose(i, b, h):
        def body(t, carry):
            at = pl.ds(pl.multiple_of(h * IMG + t * 128, 128), 128)
            v = F[i, b, at, :].T
            for hh in range(2):
                for zz in range(NZ):
                    for yy in range(NY):
                        g = (hh * NZ + zz) * NY + yy
                        to = ((zz * NY + yy) if i == 0 else (yy * NZ + zz)) * 2 + hh
                        FT[i, b, to * 16 : to * 16 + 16, at] = v[g * 16 : g * 16 + 16]
            return carry

        lax.fori_loop(0, IMG // 128, body, 0)

    def label_columns():
        for h in range(2):
            for k in range(2):
                rows = jnp.concatenate(
                    [
                        jnp.broadcast_to(LAB[h, k, 0:1, t * 128 : t * 128 + 128], (128, 128)).T
                        for t in range(IMG // 128)
                    ],
                    axis=0,
                )
                for b in range(2):
                    o = (h * 2 + k) * HALF
                    LABC[b, o : o + HALF, :] = rows[b * HALF : b * HALF + HALF] - base.astype(F32)

    def send_stats(b):
        for n, g in enumerate(group):
            push(STR.at[0, b], STR.at[slot(g), b], ss.at[b, n], sr.at[b, n], peer(g))

    def wait_stats(b):
        for n, g in enumerate(group):
            arrive(STR.at[slot(g), b], ss.at[b, n], sr.at[b, n])
    def combine(b):
        rows = []
        for i in range(2):
            vs = []
            for a in range(2):
                for n in range(4):
                    o = 4 * (i ^ a)
                    vs.append(STR[a * 4 + n, b, o : o + 4, :])
            m = functools.reduce(jnp.maximum, [v[0:1] for v in vs])
            s = s2 = 0.0
            for v in vs:
                e = jnp.exp(0.5 * (v[0:1] - m))
                s = s + v[1:2] * e
                s2 = s2 + v[2:3] * (e * e)
            per_image = (0.5 * jnp.log(s2) + 2.0 * jnp.log(s)) * 0.125
            LS[i, :, :] = LS[i] + jnp.broadcast_to(
                functools.reduce(
                    lambda p, q: p + q, [per_image[:, k * 128 : (k + 1) * 128] for k in range(GI // 128)]
                ),
                (8, 128),
            )
            rows += [m, 1.0 / s, 0.5 / s2]
        pack = jnp.concatenate(rows + rows[:2], axis=0)
        for k in range(GI // 128):
            part = pack[:, k * 128 : (k + 1) * 128]
            part = jnp.concatenate([part, jnp.zeros((120, 128), F32)], axis=0)
            COLT[k * 128 : (k + 1) * 128, :] = part.T

    R = 32

    def finish(b):
        def body(t, carry):
            at = pl.ds(pl.multiple_of(t * R, R), R)
            c = COLT[at, :]
            m0, r0, k0, m1, r1, k1 = (jnp.broadcast_to(c[:, j : j + 1], (R, 128)) for j in range(6))
            lab = jnp.broadcast_to(LABC[b, at, 0:1], (R, 128))
            lane = lax.broadcasted_iota(jnp.int32, (R, 128), 1).astype(F32)
            l0 = l1 = d0 = d1 = 0.0
            for k in range(SL // 128):
                ln = slice(k * 128, k * 128 + 128)
                x0 = X[0, b, at, ln] - m0
                x1 = X[1, b, at, ln] - m1
                e0 = jnp.exp2(x0 * HALF_LOG2E)
                e1 = jnp.exp2(x1 * HALF_LOG2E)
                s0 = e0 * r0
                s1 = e1 * r1
                q0 = s0.astype(BF16).astype(F32)
                q1 = s1.astype(BF16).astype(F32)
                hot = jnp.where(lane == lab - float(k * 128), 0.5, 0.0)
                G[0, at, ln] = (e0 * e0 * k0 - hot + (s0 - q1)).astype(BF16)
                G[1, at, ln] = (e1 * e1 * k1 - hot + (s1 - q0)).astype(BF16)
                l0 = l0 + (q1 + hot) * x0
                l1 = l1 + (q0 + hot) * x1
                d0 = d0 + (s0 - q0)
                d1 = d1 + (s1 - q1)
            l0 = l0 - m0 * d1
            l1 = l1 - m1 * d0
            LA[0, :, :] = LA[0] + fold_rows(l0)
            LA[1, :, :] = LA[1] + fold_rows(l1)
            return carry

        lax.fori_loop(0, GI // R, body, 0)

    def wgrad(i, b, start, count, rows, first):
        def body(t, carry):
            j = lax.rem(start + t, D // rows)
            at = pl.ds(pl.multiple_of(j * rows, rows), rows)
            d = jnp.dot(FT[i, b, at, :], G[i], preferred_element_type=F32)
            ACC[i, at, :] = d if first else ACC[i, at, :] + d
            return carry

        lax.fori_loop(0, count, body, 0)

    LA[...] = jnp.zeros_like(LA)
    LS[...] = jnp.zeros_like(LS)

    def wsend(kind, yy, half, o):
        push(WS.at[1, quarter(yy, half)], WS.at[1, quarter(yy, half)], ws.at[kind], wr.at[kind], ypeer(o))

    def wwait(kind, yy, half):
        arrive(WS.at[1, quarter(yy, half)], ws.at[kind], wr.at[kind])

    yd, yu, yo = lax.rem(y + NY - 1, NY), lax.rem(y + 1, NY), lax.rem(y + 2, NY)

    for c in loc:
        c.wait()
    fwait(0, 4, 0, xh, ok, 0, HALF)
    logits(0, 0, xh)
    wwait(0, y, 0)
    wsend(2, y, 0, 1)
    wwait(1, y, 1)
    wsend(4, y, 1, NY - 1)
    wsend(3, y, 1, 1)
    wsend(5, y, 0, NY - 1)
    pass_on(0)
    own_to_neighbours(1)
    transpose(0, 0, xh)
    fwait(1, 4, 0, xh, ok, 0, HALF)
    wwait(2, yd, 0)
    wsend(6, yd, 0, 1)
    wwait(4, yu, 1)
    wsend(7, yu, 1, NY - 1)
    logits(0, 1, xh)
    share_rest(0)
    transpose(0, 1, xh)
    for n, (_, bb, c) in enumerate(lab_kinds):
        arrive(LAB.at[flip(xh, bb), flip(core, c)], ls.at[n], lr.at[n])
    label_columns()
    wwait(3, yd, 1)
    wwait(5, yu, 0)
    wwait(6, yo, 0)
    wwait(7, yo, 1)
    shared_neighbours(0)
    logits(1, 0, 0)
    share_far(0)
    logits(1, 0, 1)
    shared_far(0)
    logits(0, 0, ox)
    send_stats(0)
    transpose(0, 0, ox)
    pass_on(1)
    transpose(1, 0, 0)
    transpose(1, 0, 1)
    wait_stats(0)
    combine(0)
    finish(0)
    share_rest(1)
    wgrad(0, 0, 0, 1, D, True)
    wgrad(1, 0, 0, 1, D, True)
    shared_neighbours(1)
    logits(1, 1, 0)
    logits(1, 1, 1)
    share_far(1)
    transpose(1, 1, 0)
    transpose(1, 1, 1)
    shared_far(1)
    logits(0, 1, ox)
    send_stats(1)
    transpose(0, 1, ox)
    wait_stats(1)
    combine(1)
    finish(1)

    def ring(n, me, H, chunk, S, RB, ssem, rsem, toward):
        steps = n // 2
        for t in range(steps):
            d = steps - t
            for way in range(2):
                j = lax.rem(me + (n - d if way == 0 else d), n)
                out = S[t]
                if t == 0:
                    out[way, :, :] = chunk(j, way * H, H).astype(out.dtype)
                else:
                    arrive(RB[t - 1].at[way], ssem.at[way, t - 1], rsem.at[way, t - 1])
                    if t == 1:
                        for half in range(2):
                            v = chunk(j, half * H, H)
                            if half == way:
                                v = v + RB[0][way].astype(F32)
                            out[way, half * H : half * H + H, :] = v.astype(out.dtype)
                    else:
                        v = chunk(j, 0, 2 * H) + RB[t - 1][way].astype(F32)
                        out[way, :, :] = v.astype(out.dtype)
                push(out.at[way], RB[t].at[way], ssem.at[way, t], rsem.at[way, t], toward[way])
            yield
        for way in range(2):
            arrive(RB[steps - 1].at[way], ssem.at[way, steps - 1], rsem.at[way, steps - 1])

    ydirs, zdirs = (ypeer(NY - 1), ypeer(1)), (zpeer(NZ - 1), zpeer(1))

    def acc_chunk(i, size):
        def chunk(j, lo, rows):
            return ACC[i, pl.ds(pl.multiple_of(j * size + lo, 16), rows), :]

        return chunk

    c0, c1 = D // NZ, D // NY
    r0 = ring(NZ, z, c0 // 2, acc_chunk(0, c0), S00, R00, s00s, s00r, zdirs)
    r1 = ring(NY, y, c1 // 2, acc_chunk(1, c1), S10, R10, s10s, s10r, ydirs)

    def own0():
        at = pl.ds(pl.multiple_of(z * c0, 16), c0)
        ACC[0, at, :] = ACC[0, at, :] + (R00[-1][0].astype(F32) + R00[-1][1].astype(F32))

    def own1():
        at = pl.ds(pl.multiple_of(y * c1, 16), c1)
        ACC[1, at, :] = ACC[1, at, :] + (R10[-1][0].astype(F32) + R10[-1][1].astype(F32))

    def sub_chunk(i, first):
        def chunk(j, lo, rows):
            return ACC[i, pl.ds(pl.multiple_of(first + j * 32 + lo, 16), rows), :]

        return chunk

    q0 = ring(NY, y, 16, sub_chunk(0, z * c0), S01, R01, s01s, s01r, ydirs)
    q1 = ring(NZ, z, 16, sub_chunk(1, y * c1), S11, R11, s11s, s11r, zdirs)

    def go(gen):
        for _ in gen:
            return

    wgrad(0, 1, z + NZ // 2, 1, c0, False)
    wgrad(1, 1, y + NY // 2, 1, c1, False)
    go(r0)
    go(r1)

    row = lax.broadcasted_iota(jnp.int32, (8, 128), 0)

    def put_rows(tile, r, v):
        tile = jnp.where(row == r, jnp.where(cp == 0, v[0], v[1]), tile)
        return jnp.where(row == 3 + r, jnp.where(cp == 0, v[1], v[0]), tile)

    lsums, wsums = [], []
    for i in range(2):
        wq = 0.0
        for h in range(2):
            at = pl.ds(pl.multiple_of(h * 512 + z * 64 + y * 16, 16), 16)
            wv = WS[i, at, :].astype(F32)
            wq = wq + fold_rows(fold_lanes(wv * wv))
        wsums.append(jnp.sum(wq, axis=0, keepdims=True))
        lsums.append(jnp.sum(LS[i] * 0.125 - LA[i], axis=0, keepdims=True))
    tile = put_rows(put_rows(jnp.zeros((8, 128), F32), 1, lsums), 2, wsums)

    wgrad(0, 1, z + NZ // 2 + 1, NZ - 1, c0, False)
    go(r0)
    wgrad(1, 1, y + NY // 2 + 1, NY - 1, c1, False)
    go(r1)
    go(r0)
    go(r0)
    go(r1)
    own1()
    go(q1)
    go(r0)
    own0()
    go(q0)
    go(q1)
    go(q0)
    go(q1)
    go(q0)
    go(q1)
    go(q1)

    inv = 1.0 / IMAGES
    sq = []
    for i in range(2):
        at = pl.ds(pl.multiple_of(z * c0 + y * 32 if i == 0 else y * c1 + z * 32, 32), 32)
        last = (R01 if i == 0 else R11)[-1]
        v = (ACC[i, at, :] + (last[0].astype(F32) + last[1].astype(F32))) * inv
        TB[i, :, :] = v
        sq.append(fold_rows(fold_lanes(v * v)))
    tile = put_rows(tile, 0, [jnp.sum(v, axis=0, keepdims=True) for v in sq])
    SCZ[0, :, :] = tile
    for o in range(1, NZ):
        push(SCZ.at[0], SCZ.at[o], zs.at[o - 1], zr.at[o - 1], zpeer(o))
    for n, g in enumerate(group):
        a, b, c = g
        off = pl.ds(pl.multiple_of((flip(xh, b) * 2 + flip(core, c)) * 8, 8), 8)
        push(TB.at[a, off], GB.at[:, my_s], as_.at[n], ar.at[n], peer(g))
    GB[:, my_s] = TB[0, pl.ds(pl.multiple_of((xh * 2 + core) * 8, 8), 8), :]
    for o in range(1, NZ):
        arrive(SCZ.at[o], zs.at[o - 1], zr.at[o - 1])
    SCY[0, :, :] = jnp.sum(SCZ[...], axis=0)
    for o in range(1, NY):
        push(SCY.at[0], SCY.at[o], ys.at[o - 1], yr.at[o - 1], ypeer(o))
    for o in range(1, NY):
        arrive(SCY.at[o], ys.at[o - 1], yr.at[o - 1])
    SCX[0, :, :] = jnp.sum(SCY[...], axis=0)
    for n, g in enumerate(group):
        push(SCX.at[0], SCX.at[slot(g)], xs.at[n], xr.at[n], peer(g))
    for n, g in enumerate(group):
        arrive(SCX.at[slot(g)], xs.at[n], xr.at[n])
    total = jnp.sum(SCX[...], axis=0)
    mine = jnp.where(cp == 0, total[0:3], total[3:6])
    mine = jnp.sum(mine, axis=1, keepdims=True)
    gnorm = jnp.sqrt(mine[0:1])
    wnorm = jnp.sqrt(mine[2:3])
    scale = trust * wnorm / (gnorm + decay * wnorm)
    loss_ref[...] = jnp.broadcast_to(mine[1:2] * inv, (8, 128))

    for n, (a, b, c) in enumerate(group):
        src = slice_of(flip(cp, a), flip(xh, b), flip(core, c))
        arrive(GB.at[:, src], as_.at[n], ar.at[n])
    w16 = W16[...].astype(F32)
    own_w = jnp.where(core == 0, w16[0:8], w16[8:16])
    out_ref[...] = scale * (GB[...] + decay * own_w)

    for c in sends:
        c.wait_send()


def on_device(features, labels, weight):
    lab = jnp.broadcast_to(labels.astype(F32)[None, :], (8, IMG))
    dma = pltpu.SemaphoreType.DMA
    vm = pltpu.VMEM
    any_ = pl.BlockSpec(memory_space=pl.ANY)
    ring_bufs = []
    ring_sems = []
    for rows, types in (
        (D // NZ, [BF16] * (NZ // 2 - 1) + [F32]),
        (32, [F32] * (NY // 2)),
        (D // NY, [BF16] * (NY // 2)),
        (32, [F32] * (NZ // 2)),
    ):
        bufs = tuple(vm((2, rows // 2 if t == 0 else rows, SL), dt) for t, dt in enumerate(types))
        ring_bufs += [bufs, bufs]
        ring_sems += [dma((2, len(types)))] * 2
    update, loss = pl.pallas_call(
        kernel,
        out_shape=(
            jax.ShapeDtypeStruct((8, CLASSES), F32),
            jax.ShapeDtypeStruct((8, 128), F32),
        ),
        in_specs=[any_, any_, any_],
        out_specs=(pl.BlockSpec(memory_space=vm), pl.BlockSpec(memory_space=vm)),
        scratch_shapes=[
            vm((2, 2, GI, D), BF16),
            vm((2, 2, D, GI), BF16),
            vm((2, D, SL), BF16),
            vm((16, CLASSES), BF16),
            vm((2, 2, 8, IMG), F32),
            vm((2, GI, 128), F32),
            vm((2, 2, GI, SL), F32),
            vm((2, GI, SL), BF16),
            vm((2, D, SL), F32),
            vm((8, 2, 8, GI), F32),
            vm((GI, 128), F32),
            vm((2, 8, 128), F32),
            vm((2, 8, 128), F32),
            vm((2, 32, SL), F32),
            vm((8, CLASSES), F32),
            vm((NZ, 8, 128), F32),
            vm((NY, 8, 128), F32),
            vm((8, 8, 128), F32),
            *ring_bufs,
            dma((5,)),
            dma((2, 13)), dma((2, 13)),
            dma((8,)), dma((8,)),
            dma((3,)), dma((3,)),
            dma((2, 7)), dma((2, 7)),
            dma((7,)), dma((7,)),
            dma((NZ - 1,)), dma((NZ - 1,)),
            dma((NY - 1,)), dma((NY - 1,)),
            dma((7,)), dma((7,)),
            *ring_sems,
        ],
        compiler_params=pltpu.CompilerParams(
            collective_id=0, has_side_effects=True, vmem_limit_bytes=56 * 2**20
        ),
    )(features[0], weight[0], lab)
    return (update[None], loss[0, :1])


def solution(mesh):
    placed = (P("copy", "dp", None), P("dp"), P("copy", None, None))
    return jax.shard_map(
        on_device,
        mesh=mesh,
        in_specs=placed,
        out_specs=(P("copy", "dp", None), P("copy")),
        check_vma=False,
    )
```

```python
import functools

import jax
import jax.numpy as jnp
import numpy as np
from jax import lax
from jax.experimental import pallas as pl
from jax.experimental.pallas import tpu as pltpu
from jax.sharding import PartitionSpec as P

MESH = pl.DeviceIdType.MESH
NZ, NY = 8, 4
IMG = 384
D = 1024
CLASSES = 5120
SL = CLASSES // 8
IMAGES = 49152
HALF = IMG // 2
GI = 2 * IMG
HALF_LOG2E = 0.5 * float(np.log2(np.e))
trust = 32.0
decay = 5e-05
F32, BF16 = jnp.float32, jnp.bfloat16


def fold_lanes(v):
    out = v[:, 0:128]
    for k in range(1, SL // 128):
        out = out + v[:, k * 128 : (k + 1) * 128]
    return out


def fold_rows(v):
    out = v[0:8]
    for k in range(1, v.shape[0] // 8):
        out = out + v[k * 8 : (k + 1) * 8]
    return out


def kernel(
    f_in, w_in, lab_in,
    out_ref, loss_ref,
    F, FT, WS, W16, LAB, LABC, X, G, ACC, STR, COLT, LA, LS, TB, GB,
    SCZ, SCY, SCX,
    S00, R00, S01, R01, S10, R10, S11, R11,
    loc_sem, fs, fr, ws, wr, ls, lr, ss, sr, as_, ar,
    zs, zr, ys, yr, xs, xr,
    s00s, s00r, s01s, s01r, s10s, s10r, s11s, s11r,
):
    cp = lax.axis_index("copy")
    dp = lax.axis_index("dp")
    core = lax.rem(dp, 2)
    y = lax.rem(dp // 2, NY)
    z = lax.rem(dp // (2 * NY), NZ)
    xh = dp // (2 * NY * NZ)
    oc, ox, ok = 1 - cp, 1 - xh, 1 - core

    def dev(c, h, zz, yy, k):
        return (c, ((h * NZ + zz) * NY + yy) * 2 + k)

    partner = dev(oc, xh, z, y, core)
    nonp = dev(oc, ox, z, y, core)
    sib = dev(cp, xh, z, y, ok)

    def flip(v, bit):
        return 1 - v if bit else v

    group = [(a, b, c) for a in range(2) for b in range(2) for c in range(2)][1:]

    def peer(abc):
        a, b, c = abc
        return dev(flip(cp, a), flip(xh, b), z, y, flip(core, c))

    def slot(abc):
        return abc[0] * 4 + abc[1] * 2 + abc[2]

    def ypeer(o):
        return dev(cp, xh, z, lax.rem(y + o, NY), core)

    def zpeer(o):
        return dev(cp, xh, lax.rem(z + o, NZ), y, core)

    def slice_of(c, h, k):
        return pl.ds(pl.multiple_of(((c * 2 + h) * 2 + k) * SL, 128), SL)

    my_s = slice_of(cp, xh, core)
    base = ((cp * 2 + xh) * 2 + core) * SL

    def block(h, k, lo, rows):
        return pl.ds(pl.multiple_of((h * 2 + k) * HALF + lo, 16), rows)

    loc = [
        pltpu.make_async_copy(
            f_in.at[pl.ds(b * HALF, HALF)], F.at[0, b, block(xh, core, 0, HALF)], loc_sem.at[b]
        )
        for b in range(2)
    ] + [
        pltpu.make_async_copy(w_in.at[:, my_s], WS.at[0], loc_sem.at[2]),
        pltpu.make_async_copy(
            w_in.at[pl.ds(pl.multiple_of((dp // 2) * 16, 16), 16), :], W16, loc_sem.at[3]
        ),
        pltpu.make_async_copy(lab_in, LAB.at[xh, core], loc_sem.at[4]),
    ]
    for c in loc:
        c.start()

    peers = [peer(g) for g in group] + [ypeer(o) for o in range(1, NY)] + [zpeer(o) for o in range(1, NZ)]
    barrier = pltpu.get_barrier_semaphore()
    for p in peers:
        pl.semaphore_signal(barrier, inc=1, device_id=p, device_id_type=MESH)
    pl.semaphore_wait(barrier, len(peers))

    sends = []

    def remote(src, dst, s, r, to):
        c = pltpu.make_async_remote_copy(
            src_ref=src, dst_ref=dst, send_sem=s, recv_sem=r, device_id=to, device_id_type=MESH
        )
        return c

    def push(src, dst, s, r, to):
        c = remote(src, dst, s, r, to)
        c.start()
        sends.append(c)

    def arrive(ref, s, r):
        remote(ref, ref, s, r, partner).wait_recv()

    def quarter(yy, h):
        return pl.ds(pl.multiple_of((yy * 2 + h) * (D // NY // 2), 64), D // NY // 2)

    push(w_in.at[quarter(y, 0), slice_of(oc, xh, core)], WS.at[1, quarter(y, 0)], ws.at[0], wr.at[0], partner)
    push(w_in.at[quarter(y, 1), slice_of(oc, ox, core)], WS.at[1, quarter(y, 1)], ws.at[1], wr.at[1], nonp)

    PART = HALF // 2
    LO, HI = 0, PART

    def fpush(b, kind, own, i, h, k, lo, rows, to, src_i=None):
        at = block(h, k, lo, rows)
        src = f_in.at[pl.ds(b * HALF + lo, rows)] if own else F.at[i if src_i is None else src_i, b, at]
        push(src, F.at[i, b, at], fs.at[b, kind], fr.at[b, kind], to)

    def fwait(b, kind, i, h, k, lo, rows=PART):
        arrive(F.at[i, b, block(h, k, lo, rows)], fs.at[b, kind], fr.at[b, kind])

    def own_to_neighbours(b):
        fpush(b, 0, True, 1, xh, core, LO, PART, partner)
        fpush(b, 2, True, 1, xh, core, HI, PART, nonp)
        fpush(b, 1, True, 1, xh, core, HI, PART, partner)
        fpush(b, 3, True, 1, xh, core, LO, PART, nonp)

    def pass_on(b):
        fwait(b, 0, 1, xh, core, LO)
        fpush(b, 5, False, 0, xh, core, LO, PART, nonp, 1)
        fwait(b, 2, 1, ox, core, HI)
        fpush(b, 6, False, 0, ox, core, HI, PART, partner, 1)
        fpush(b, 7, False, 1, xh, core, LO, PART, sib)
        fpush(b, 9, False, 1, ox, core, HI, PART, sib)

    def share_rest(b):
        fwait(b, 1, 1, xh, core, HI)
        fpush(b, 8, False, 1, xh, core, HI, PART, sib)
        fwait(b, 3, 1, ox, core, LO)
        fpush(b, 10, False, 1, ox, core, LO, PART, sib)

    def share_far(b):
        fwait(b, 5, 0, ox, core, LO)
        fpush(b, 11, False, 0, ox, core, LO, PART, sib)
        fwait(b, 6, 0, ox, core, HI)
        fpush(b, 12, False, 0, ox, core, HI, PART, sib)

    def shared_neighbours(b):
        fwait(b, 7, 1, xh, ok, LO)
        fwait(b, 9, 1, ox, ok, HI)
        fwait(b, 8, 1, xh, ok, HI)
        fwait(b, 10, 1, ox, ok, LO)

    def shared_far(b):
        fwait(b, 11, 0, ox, ok, LO)
        fwait(b, 12, 0, ox, ok, HI)

    own_to_neighbours(0)
    for b in range(2):
        fpush(b, 4, True, 0, xh, core, 0, HALF, sib)

    lab_kinds = [(0, 0, 1), (0, 1, 0), (0, 1, 1)]
    for n, g in enumerate(lab_kinds):
        push(lab_in, LAB.at[xh, core], ls.at[n], lr.at[n], peer(g))

    def logits(i, b, h):
        rows = pl.ds(pl.multiple_of(h * IMG, 128), IMG)
        X[i, b, rows, :] = jnp.dot(F[i, b, rows, :], WS[i], preferred_element_type=F32)

        def body(t, carry):
            at = pl.ds(pl.multiple_of(h * IMG + t * 128, 128), 128)
            lg = [X[i, b, at, k * 128 : k * 128 + 128] for k in range(SL // 128)]
            m = jnp.max(functools.reduce(jnp.maximum, lg), axis=1, keepdims=True)
            s = s2 = 0.0
            for v in lg:
                e = jnp.exp2((v - m) * HALF_LOG2E)
                s = s + e
                s2 = s2 + e * e
            s = jnp.sum(s, axis=1, keepdims=True)
            s2 = jnp.sum(s2, axis=1, keepdims=True)
            lane = lax.broadcasted_iota(jnp.int32, (128, 128), 1)
            tile = jnp.where(lane == 0, m, jnp.where(lane == 1, s, s2))
            STR[0, b, 4 * i : 4 * i + 4, at] = tile.T[0:4]
            return carry

        lax.fori_loop(0, IMG // 128, body, 0, unroll=True)

    def transpose(i, b, h):
        def body(t, carry):
            at = pl.ds(pl.multiple_of(h * IMG + t * 128, 128), 128)
            v = F[i, b, at, :].T
            for hh in range(2):
                for zz in range(NZ):
                    for yy in range(NY):
                        g = (hh * NZ + zz) * NY + yy
                        to = ((zz * NY + yy) if i == 0 else (yy * NZ + zz)) * 2 + hh
                        FT[i, b, to * 16 : to * 16 + 16, at] = v[g * 16 : g * 16 + 16]
            return carry

        lax.fori_loop(0, IMG // 128, body, 0)

    def label_columns():
        for h in range(2):
            for k in range(2):
                rows = jnp.concatenate(
                    [
                        jnp.broadcast_to(LAB[h, k, 0:1, t * 128 : t * 128 + 128], (128, 128)).T
                        for t in range(IMG // 128)
                    ],
                    axis=0,
                )
                for b in range(2):
                    o = (h * 2 + k) * HALF
                    LABC[b, o : o + HALF, :] = rows[b * HALF : b * HALF + HALF] - base.astype(F32)

    def send_stats(b):
        for n, g in enumerate(group):
            push(STR.at[0, b], STR.at[slot(g), b], ss.at[b, n], sr.at[b, n], peer(g))

    def wait_stats(b):
        for n, g in enumerate(group):
            arrive(STR.at[slot(g), b], ss.at[b, n], sr.at[b, n])
    def combine(b):
        rows = []
        for i in range(2):
            vs = []
            for a in range(2):
                for n in range(4):
                    o = 4 * (i ^ a)
                    vs.append(STR[a * 4 + n, b, o : o + 4, :])
            m = functools.reduce(jnp.maximum, [v[0:1] for v in vs])
            s = s2 = 0.0
            for v in vs:
                e = jnp.exp(0.5 * (v[0:1] - m))
                s = s + v[1:2] * e
                s2 = s2 + v[2:3] * (e * e)
            per_image = (0.5 * jnp.log(s2) + 2.0 * jnp.log(s)) * 0.125
            LS[i, :, :] = LS[i] + jnp.broadcast_to(
                functools.reduce(
                    lambda p, q: p + q, [per_image[:, k * 128 : (k + 1) * 128] for k in range(GI // 128)]
                ),
                (8, 128),
            )
            rows += [m, 1.0 / s, 0.5 / s2]
        pack = jnp.concatenate(rows + rows[:2], axis=0)
        for k in range(GI // 128):
            part = pack[:, k * 128 : (k + 1) * 128]
            part = jnp.concatenate([part, jnp.zeros((120, 128), F32)], axis=0)
            COLT[k * 128 : (k + 1) * 128, :] = part.T

    R = 32

    def finish(b):
        def body(t, carry):
            at = pl.ds(pl.multiple_of(t * R, R), R)
            c = COLT[at, :]
            m0, r0, k0, m1, r1, k1 = (jnp.broadcast_to(c[:, j : j + 1], (R, 128)) for j in range(6))
            lab = jnp.broadcast_to(LABC[b, at, 0:1], (R, 128))
            lane = lax.broadcasted_iota(jnp.int32, (R, 128), 1).astype(F32)
            l0 = l1 = d0 = d1 = 0.0
            for k in range(SL // 128):
                ln = slice(k * 128, k * 128 + 128)
                x0 = X[0, b, at, ln] - m0
                x1 = X[1, b, at, ln] - m1
                e0 = jnp.exp2(x0 * HALF_LOG2E)
                e1 = jnp.exp2(x1 * HALF_LOG2E)
                s0 = e0 * r0
                s1 = e1 * r1
                q0 = s0.astype(BF16).astype(F32)
                q1 = s1.astype(BF16).astype(F32)
                hot = jnp.where(lane == lab - float(k * 128), 0.5, 0.0)
                G[0, at, ln] = (e0 * e0 * k0 - hot + (s0 - q1)).astype(BF16)
                G[1, at, ln] = (e1 * e1 * k1 - hot + (s1 - q0)).astype(BF16)
                l0 = l0 + (q1 + hot) * x0
                l1 = l1 + (q0 + hot) * x1
                d0 = d0 + (s0 - q0)
                d1 = d1 + (s1 - q1)
            l0 = l0 - m0 * d1
            l1 = l1 - m1 * d0
            LA[0, :, :] = LA[0] + fold_rows(l0)
            LA[1, :, :] = LA[1] + fold_rows(l1)
            return carry

        lax.fori_loop(0, GI // R, body, 0)

    def wgrad(i, b, start, count, rows, first):
        def body(t, carry):
            j = lax.rem(start + t, D // rows)
            at = pl.ds(pl.multiple_of(j * rows, rows), rows)
            d = jnp.dot(FT[i, b, at, :], G[i], preferred_element_type=F32)
            ACC[i, at, :] = d if first else ACC[i, at, :] + d
            return carry

        lax.fori_loop(0, count, body, 0)

    LA[...] = jnp.zeros_like(LA)
    LS[...] = jnp.zeros_like(LS)

    def wsend(kind, yy, half, o):
        push(WS.at[1, quarter(yy, half)], WS.at[1, quarter(yy, half)], ws.at[kind], wr.at[kind], ypeer(o))

    def wwait(kind, yy, half):
        arrive(WS.at[1, quarter(yy, half)], ws.at[kind], wr.at[kind])

    yd, yu, yo = lax.rem(y + NY - 1, NY), lax.rem(y + 1, NY), lax.rem(y + 2, NY)

    for c in loc:
        c.wait()
    fwait(0, 4, 0, xh, ok, 0, HALF)
    logits(0, 0, xh)
    wwait(0, y, 0)
    wsend(2, y, 0, 1)
    wwait(1, y, 1)
    wsend(4, y, 1, NY - 1)
    wsend(3, y, 1, 1)
    wsend(5, y, 0, NY - 1)
    pass_on(0)
    own_to_neighbours(1)
    transpose(0, 0, xh)
    fwait(1, 4, 0, xh, ok, 0, HALF)
    wwait(2, yd, 0)
    wsend(6, yd, 0, 1)
    wwait(4, yu, 1)
    wsend(7, yu, 1, NY - 1)
    logits(0, 1, xh)
    share_rest(0)
    transpose(0, 1, xh)
    for n, (_, bb, c) in enumerate(lab_kinds):
        arrive(LAB.at[flip(xh, bb), flip(core, c)], ls.at[n], lr.at[n])
    label_columns()
    wwait(3, yd, 1)
    wwait(5, yu, 0)
    wwait(6, yo, 0)
    wwait(7, yo, 1)
    shared_neighbours(0)
    logits(1, 0, 0)
    share_far(0)
    logits(1, 0, 1)
    shared_far(0)
    logits(0, 0, ox)
    send_stats(0)
    transpose(0, 0, ox)
    pass_on(1)
    transpose(1, 0, 0)
    transpose(1, 0, 1)
    wait_stats(0)
    combine(0)
    finish(0)
    share_rest(1)
    shared_neighbours(1)
    logits(1, 1, 0)
    logits(1, 1, 1)
    share_far(1)
    transpose(1, 1, 0)
    transpose(1, 1, 1)
    shared_far(1)
    logits(0, 1, ox)
    send_stats(1)
    transpose(0, 1, ox)
    wgrad(0, 0, 0, 1, D, True)
    wgrad(1, 0, 0, 1, D, True)
    wait_stats(1)
    combine(1)
    finish(1)

    def ring(n, me, H, chunk, S, RB, ssem, rsem, toward):
        steps = n // 2
        for t in range(steps):
            d = steps - t
            for way in range(2):
                j = lax.rem(me + (n - d if way == 0 else d), n)
                out = S[t]
                if t == 0:
                    out[way, :, :] = chunk(j, way * H, H).astype(out.dtype)
                else:
                    arrive(RB[t - 1].at[way], ssem.at[way, t - 1], rsem.at[way, t - 1])
                    if t == 1:
                        for half in range(2):
                            v = chunk(j, half * H, H)
                            if half == way:
                                v = v + RB[0][way].astype(F32)
                            out[way, half * H : half * H + H, :] = v.astype(out.dtype)
                    else:
                        v = chunk(j, 0, 2 * H) + RB[t - 1][way].astype(F32)
                        out[way, :, :] = v.astype(out.dtype)
                push(out.at[way], RB[t].at[way], ssem.at[way, t], rsem.at[way, t], toward[way])
            yield
        for way in range(2):
            arrive(RB[steps - 1].at[way], ssem.at[way, steps - 1], rsem.at[way, steps - 1])

    ydirs, zdirs = (ypeer(NY - 1), ypeer(1)), (zpeer(NZ - 1), zpeer(1))

    def acc_chunk(i, size):
        def chunk(j, lo, rows):
            return ACC[i, pl.ds(pl.multiple_of(j * size + lo, 16), rows), :]

        return chunk

    c0, c1 = D // NZ, D // NY
    r0 = ring(NZ, z, c0 // 2, acc_chunk(0, c0), S00, R00, s00s, s00r, zdirs)
    r1 = ring(NY, y, c1 // 2, acc_chunk(1, c1), S10, R10, s10s, s10r, ydirs)

    def own0():
        at = pl.ds(pl.multiple_of(z * c0, 16), c0)
        ACC[0, at, :] = ACC[0, at, :] + (R00[-1][0].astype(F32) + R00[-1][1].astype(F32))

    def own1():
        at = pl.ds(pl.multiple_of(y * c1, 16), c1)
        ACC[1, at, :] = ACC[1, at, :] + (R10[-1][0].astype(F32) + R10[-1][1].astype(F32))

    def sub_chunk(i, first):
        def chunk(j, lo, rows):
            return ACC[i, pl.ds(pl.multiple_of(first + j * 32 + lo, 16), rows), :]

        return chunk

    q0 = ring(NY, y, 16, sub_chunk(0, z * c0), S01, R01, s01s, s01r, ydirs)
    q1 = ring(NZ, z, 16, sub_chunk(1, y * c1), S11, R11, s11s, s11r, zdirs)

    def go(gen):
        for _ in gen:
            return

    wgrad(0, 1, z + NZ // 2, 1, c0, False)
    wgrad(1, 1, y + NY // 2, 1, c1, False)
    go(r0)
    go(r1)

    row = lax.broadcasted_iota(jnp.int32, (8, 128), 0)

    def put_rows(tile, r, v):
        tile = jnp.where(row == r, jnp.where(cp == 0, v[0], v[1]), tile)
        return jnp.where(row == 3 + r, jnp.where(cp == 0, v[1], v[0]), tile)

    lsums, wsums = [], []
    for i in range(2):
        wq = 0.0
        for h in range(2):
            at = pl.ds(pl.multiple_of(h * 512 + z * 64 + y * 16, 16), 16)
            wv = WS[i, at, :].astype(F32)
            wq = wq + fold_rows(fold_lanes(wv * wv))
        wsums.append(jnp.sum(wq, axis=0, keepdims=True))
        lsums.append(jnp.sum(LS[i] * 0.125 - LA[i], axis=0, keepdims=True))
    tile = put_rows(put_rows(jnp.zeros((8, 128), F32), 1, lsums), 2, wsums)

    wgrad(0, 1, z + NZ // 2 + 1, NZ - 1, c0, False)
    go(r0)
    wgrad(1, 1, y + NY // 2 + 1, NY - 1, c1, False)
    go(r1)
    go(r0)
    go(r0)
    go(r1)
    own1()
    go(q1)
    go(r0)
    own0()
    go(q0)
    go(q1)
    go(q0)
    go(q1)
    go(q0)
    go(q1)
    go(q1)

    inv = 1.0 / IMAGES
    sq = []
    for i in range(2):
        at = pl.ds(pl.multiple_of(z * c0 + y * 32 if i == 0 else y * c1 + z * 32, 32), 32)
        last = (R01 if i == 0 else R11)[-1]
        v = (ACC[i, at, :] + (last[0].astype(F32) + last[1].astype(F32))) * inv
        TB[i, :, :] = v
        sq.append(fold_rows(fold_lanes(v * v)))
    tile = put_rows(tile, 0, [jnp.sum(v, axis=0, keepdims=True) for v in sq])
    SCZ[0, :, :] = tile
    for o in range(1, NZ):
        push(SCZ.at[0], SCZ.at[o], zs.at[o - 1], zr.at[o - 1], zpeer(o))
    for n, g in enumerate(group):
        a, b, c = g
        off = pl.ds(pl.multiple_of((flip(xh, b) * 2 + flip(core, c)) * 8, 8), 8)
        push(TB.at[a, off], GB.at[:, my_s], as_.at[n], ar.at[n], peer(g))
    GB[:, my_s] = TB[0, pl.ds(pl.multiple_of((xh * 2 + core) * 8, 8), 8), :]
    for o in range(1, NZ):
        arrive(SCZ.at[o], zs.at[o - 1], zr.at[o - 1])
    SCY[0, :, :] = jnp.sum(SCZ[...], axis=0)
    for o in range(1, NY):
        push(SCY.at[0], SCY.at[o], ys.at[o - 1], yr.at[o - 1], ypeer(o))
    for o in range(1, NY):
        arrive(SCY.at[o], ys.at[o - 1], yr.at[o - 1])
    SCX[0, :, :] = jnp.sum(SCY[...], axis=0)
    for n, g in enumerate(group):
        push(SCX.at[0], SCX.at[slot(g)], xs.at[n], xr.at[n], peer(g))
    for n, g in enumerate(group):
        arrive(SCX.at[slot(g)], xs.at[n], xr.at[n])
    total = jnp.sum(SCX[...], axis=0)
    mine = jnp.where(cp == 0, total[0:3], total[3:6])
    mine = jnp.sum(mine, axis=1, keepdims=True)
    gnorm = jnp.sqrt(mine[0:1])
    wnorm = jnp.sqrt(mine[2:3])
    scale = trust * wnorm / (gnorm + decay * wnorm)
    loss_ref[...] = jnp.broadcast_to(mine[1:2] * inv, (8, 128))

    for n, (a, b, c) in enumerate(group):
        src = slice_of(flip(cp, a), flip(xh, b), flip(core, c))
        arrive(GB.at[:, src], as_.at[n], ar.at[n])
    w16 = W16[...].astype(F32)
    own_w = jnp.where(core == 0, w16[0:8], w16[8:16])
    out_ref[...] = scale * (GB[...] + decay * own_w)

    for c in sends:
        c.wait_send()


def on_device(features, labels, weight):
    lab = jnp.broadcast_to(labels.astype(F32)[None, :], (8, IMG))
    dma = pltpu.SemaphoreType.DMA
    vm = pltpu.VMEM
    any_ = pl.BlockSpec(memory_space=pl.ANY)
    ring_bufs = []
    ring_sems = []
    for rows, types in (
        (D // NZ, [BF16] * (NZ // 2 - 1) + [F32]),
        (32, [F32] * (NY // 2)),
        (D // NY, [BF16] * (NY // 2)),
        (32, [F32] * (NZ // 2)),
    ):
        bufs = tuple(vm((2, rows // 2 if t == 0 else rows, SL), dt) for t, dt in enumerate(types))
        ring_bufs += [bufs, bufs]
        ring_sems += [dma((2, len(types)))] * 2
    update, loss = pl.pallas_call(
        kernel,
        out_shape=(
            jax.ShapeDtypeStruct((8, CLASSES), F32),
            jax.ShapeDtypeStruct((8, 128), F32),
        ),
        in_specs=[any_, any_, any_],
        out_specs=(pl.BlockSpec(memory_space=vm), pl.BlockSpec(memory_space=vm)),
        scratch_shapes=[
            vm((2, 2, GI, D), BF16),
            vm((2, 2, D, GI), BF16),
            vm((2, D, SL), BF16),
            vm((16, CLASSES), BF16),
            vm((2, 2, 8, IMG), F32),
            vm((2, GI, 128), F32),
            vm((2, 2, GI, SL), F32),
            vm((2, GI, SL), BF16),
            vm((2, D, SL), F32),
            vm((8, 2, 8, GI), F32),
            vm((GI, 128), F32),
            vm((2, 8, 128), F32),
            vm((2, 8, 128), F32),
            vm((2, 32, SL), F32),
            vm((8, CLASSES), F32),
            vm((NZ, 8, 128), F32),
            vm((NY, 8, 128), F32),
            vm((8, 8, 128), F32),
            *ring_bufs,
            dma((5,)),
            dma((2, 13)), dma((2, 13)),
            dma((8,)), dma((8,)),
            dma((3,)), dma((3,)),
            dma((2, 7)), dma((2, 7)),
            dma((7,)), dma((7,)),
            dma((NZ - 1,)), dma((NZ - 1,)),
            dma((NY - 1,)), dma((NY - 1,)),
            dma((7,)), dma((7,)),
            *ring_sems,
        ],
        compiler_params=pltpu.CompilerParams(
            collective_id=0, has_side_effects=True, vmem_limit_bytes=56 * 2**20
        ),
    )(features[0], weight[0], lab)
    return (update[None], loss[0, :1])


def solution(mesh):
    placed = (P("copy", "dp", None), P("dp"), P("copy", None, None))
    return jax.shard_map(
        on_device,
        mesh=mesh,
        in_specs=placed,
        out_specs=(P("copy", "dp", None), P("copy")),
        check_vma=False,
    )
```

```python
import functools

import jax
import jax.numpy as jnp
import numpy as np
from jax import lax
from jax.experimental import pallas as pl
from jax.experimental.pallas import tpu as pltpu
from jax.sharding import PartitionSpec as P

MESH = pl.DeviceIdType.MESH
NZ, NY = 8, 4
IMG = 384
D = 1024
CLASSES = 5120
SL = CLASSES // 8
IMAGES = 49152
HALF = IMG // 2
GI = 2 * IMG
HALF_LOG2E = 0.5 * float(np.log2(np.e))
trust = 32.0
decay = 5e-05
F32, BF16 = jnp.float32, jnp.bfloat16


def fold_lanes(v):
    out = v[:, 0:128]
    for k in range(1, SL // 128):
        out = out + v[:, k * 128 : (k + 1) * 128]
    return out


def fold_rows(v):
    out = v[0:8]
    for k in range(1, v.shape[0] // 8):
        out = out + v[k * 8 : (k + 1) * 8]
    return out


def kernel(
    f_in, w_in, lab_in,
    out_ref, loss_ref,
    F, FT, WS, W16, LAB, LABC, X, G, ACC, STR, COLT, LA, LS, TB, GB,
    SCZ, SCY, SCX,
    S00, R00, S01, R01, S10, R10, S11, R11,
    loc_sem, fs, fr, ws, wr, ls, lr, ss, sr, as_, ar,
    zs, zr, ys, yr, xs, xr,
    s00s, s00r, s01s, s01r, s10s, s10r, s11s, s11r,
):
    cp = lax.axis_index("copy")
    dp = lax.axis_index("dp")
    core = lax.rem(dp, 2)
    y = lax.rem(dp // 2, NY)
    z = lax.rem(dp // (2 * NY), NZ)
    xh = dp // (2 * NY * NZ)
    oc, ox, ok = 1 - cp, 1 - xh, 1 - core

    def dev(c, h, zz, yy, k):
        return (c, ((h * NZ + zz) * NY + yy) * 2 + k)

    partner = dev(oc, xh, z, y, core)
    nonp = dev(oc, ox, z, y, core)
    sib = dev(cp, xh, z, y, ok)

    def flip(v, bit):
        return 1 - v if bit else v

    group = [(a, b, c) for a in range(2) for b in range(2) for c in range(2)][1:]

    def peer(abc):
        a, b, c = abc
        return dev(flip(cp, a), flip(xh, b), z, y, flip(core, c))

    def slot(abc):
        return abc[0] * 4 + abc[1] * 2 + abc[2]

    def ypeer(o):
        return dev(cp, xh, z, lax.rem(y + o, NY), core)

    def zpeer(o):
        return dev(cp, xh, lax.rem(z + o, NZ), y, core)

    def slice_of(c, h, k):
        return pl.ds(pl.multiple_of(((c * 2 + h) * 2 + k) * SL, 128), SL)

    my_s = slice_of(cp, xh, core)
    base = ((cp * 2 + xh) * 2 + core) * SL

    def block(h, k, lo, rows):
        return pl.ds(pl.multiple_of((h * 2 + k) * HALF + lo, 16), rows)

    loc = [
        pltpu.make_async_copy(
            f_in.at[pl.ds(b * HALF, HALF)], F.at[0, b, block(xh, core, 0, HALF)], loc_sem.at[b]
        )
        for b in range(2)
    ] + [
        pltpu.make_async_copy(w_in.at[:, my_s], WS.at[0], loc_sem.at[2]),
        pltpu.make_async_copy(
            w_in.at[pl.ds(pl.multiple_of((dp // 2) * 16, 16), 16), :], W16, loc_sem.at[3]
        ),
        pltpu.make_async_copy(lab_in, LAB.at[xh, core], loc_sem.at[4]),
    ]
    for c in loc:
        c.start()

    peers = [peer(g) for g in group] + [ypeer(o) for o in range(1, NY)] + [zpeer(o) for o in range(1, NZ)]
    barrier = pltpu.get_barrier_semaphore()
    for p in peers:
        pl.semaphore_signal(barrier, inc=1, device_id=p, device_id_type=MESH)
    pl.semaphore_wait(barrier, len(peers))

    sends = []

    def remote(src, dst, s, r, to):
        c = pltpu.make_async_remote_copy(
            src_ref=src, dst_ref=dst, send_sem=s, recv_sem=r, device_id=to, device_id_type=MESH
        )
        return c

    def push(src, dst, s, r, to):
        c = remote(src, dst, s, r, to)
        c.start()
        sends.append(c)

    def arrive(ref, s, r):
        remote(ref, ref, s, r, partner).wait_recv()

    def quarter(yy, h):
        return pl.ds(pl.multiple_of((yy * 2 + h) * (D // NY // 2), 64), D // NY // 2)

    push(w_in.at[quarter(y, 0), slice_of(oc, xh, core)], WS.at[1, quarter(y, 0)], ws.at[0], wr.at[0], partner)
    push(w_in.at[quarter(y, 1), slice_of(oc, ox, core)], WS.at[1, quarter(y, 1)], ws.at[1], wr.at[1], nonp)

    PART = HALF // 2
    LO, HI = 0, PART

    def fpush(b, kind, own, i, h, k, lo, rows, to, src_i=None):
        at = block(h, k, lo, rows)
        src = f_in.at[pl.ds(b * HALF + lo, rows)] if own else F.at[i if src_i is None else src_i, b, at]
        push(src, F.at[i, b, at], fs.at[b, kind], fr.at[b, kind], to)

    def fwait(b, kind, i, h, k, lo, rows=PART):
        arrive(F.at[i, b, block(h, k, lo, rows)], fs.at[b, kind], fr.at[b, kind])

    def own_to_neighbours(b):
        fpush(b, 0, True, 1, xh, core, LO, PART, partner)
        fpush(b, 2, True, 1, xh, core, HI, PART, nonp)
        fpush(b, 1, True, 1, xh, core, HI, PART, partner)
        fpush(b, 3, True, 1, xh, core, LO, PART, nonp)

    def pass_on(b):
        fwait(b, 0, 1, xh, core, LO)
        fpush(b, 5, False, 0, xh, core, LO, PART, nonp, 1)
        fwait(b, 2, 1, ox, core, HI)
        fpush(b, 6, False, 0, ox, core, HI, PART, partner, 1)
        fpush(b, 7, False, 1, xh, core, LO, PART, sib)
        fpush(b, 9, False, 1, ox, core, HI, PART, sib)

    def share_rest(b):
        fwait(b, 1, 1, xh, core, HI)
        fpush(b, 8, False, 1, xh, core, HI, PART, sib)
        fwait(b, 3, 1, ox, core, LO)
        fpush(b, 10, False, 1, ox, core, LO, PART, sib)

    def share_far(b):
        fwait(b, 5, 0, ox, core, LO)
        fpush(b, 11, False, 0, ox, core, LO, PART, sib)
        fwait(b, 6, 0, ox, core, HI)
        fpush(b, 12, False, 0, ox, core, HI, PART, sib)

    def shared_neighbours(b):
        fwait(b, 7, 1, xh, ok, LO)
        fwait(b, 9, 1, ox, ok, HI)
        fwait(b, 8, 1, xh, ok, HI)
        fwait(b, 10, 1, ox, ok, LO)

    def shared_far(b):
        fwait(b, 11, 0, ox, ok, LO)
        fwait(b, 12, 0, ox, ok, HI)

    own_to_neighbours(0)
    for b in range(2):
        fpush(b, 4, True, 0, xh, core, 0, HALF, sib)

    lab_kinds = [(0, 0, 1), (0, 1, 0), (0, 1, 1)]
    for n, g in enumerate(lab_kinds):
        push(lab_in, LAB.at[xh, core], ls.at[n], lr.at[n], peer(g))

    def logits(i, b, h):
        rows = pl.ds(pl.multiple_of(h * IMG, 128), IMG)
        X[i, b, rows, :] = jnp.dot(F[i, b, rows, :], WS[i], preferred_element_type=F32)

        def body(t, carry):
            at = pl.ds(pl.multiple_of(h * IMG + t * 128, 128), 128)
            lg = [X[i, b, at, k * 128 : k * 128 + 128] for k in range(SL // 128)]
            m = jnp.max(functools.reduce(jnp.maximum, lg), axis=1, keepdims=True)
            s = s2 = 0.0
            for v in lg:
                e = jnp.exp2((v - m) * HALF_LOG2E)
                s = s + e
                s2 = s2 + e * e
            s = jnp.sum(s, axis=1, keepdims=True)
            s2 = jnp.sum(s2, axis=1, keepdims=True)
            lane = lax.broadcasted_iota(jnp.int32, (128, 128), 1)
            tile = jnp.where(lane == 0, m, jnp.where(lane == 1, s, s2))
            STR[0, b, 4 * i : 4 * i + 4, at] = tile.T[0:4]
            return carry

        lax.fori_loop(0, IMG // 128, body, 0, unroll=True)

    def transpose(i, b, h):
        def body(t, carry):
            at = pl.ds(pl.multiple_of(h * IMG + t * 128, 128), 128)
            v = F[i, b, at, :].T
            for hh in range(2):
                for zz in range(NZ):
                    for yy in range(NY):
                        g = (hh * NZ + zz) * NY + yy
                        to = ((zz * NY + yy) if i == 0 else (yy * NZ + zz)) * 2 + hh
                        FT[i, b, to * 16 : to * 16 + 16, at] = v[g * 16 : g * 16 + 16]
            return carry

        lax.fori_loop(0, IMG // 128, body, 0)

    def label_columns():
        for h in range(2):
            for k in range(2):
                rows = jnp.concatenate(
                    [
                        jnp.broadcast_to(LAB[h, k, 0:1, t * 128 : t * 128 + 128], (128, 128)).T
                        for t in range(IMG // 128)
                    ],
                    axis=0,
                )
                for b in range(2):
                    o = (h * 2 + k) * HALF
                    LABC[b, o : o + HALF, :] = rows[b * HALF : b * HALF + HALF] - base.astype(F32)

    def send_stats(b):
        for n, g in enumerate(group):
            push(STR.at[0, b], STR.at[slot(g), b], ss.at[b, n], sr.at[b, n], peer(g))

    def wait_stats(b):
        for n, g in enumerate(group):
            arrive(STR.at[slot(g), b], ss.at[b, n], sr.at[b, n])
    def combine(b):
        rows = []
        for i in range(2):
            vs = []
            for a in range(2):
                for n in range(4):
                    o = 4 * (i ^ a)
                    vs.append(STR[a * 4 + n, b, o : o + 4, :])
            m = functools.reduce(jnp.maximum, [v[0:1] for v in vs])
            s = s2 = 0.0
            for v in vs:
                e = jnp.exp(0.5 * (v[0:1] - m))
                s = s + v[1:2] * e
                s2 = s2 + v[2:3] * (e * e)
            per_image = (0.5 * jnp.log(s2) + 2.0 * jnp.log(s)) * 0.125
            LS[i, :, :] = LS[i] + jnp.broadcast_to(
                functools.reduce(
                    lambda p, q: p + q, [per_image[:, k * 128 : (k + 1) * 128] for k in range(GI // 128)]
                ),
                (8, 128),
            )
            rows += [m, 1.0 / s, 0.5 / s2]
        pack = jnp.concatenate(rows + rows[:2], axis=0)
        for k in range(GI // 128):
            part = pack[:, k * 128 : (k + 1) * 128]
            part = jnp.concatenate([part, jnp.zeros((120, 128), F32)], axis=0)
            COLT[k * 128 : (k + 1) * 128, :] = part.T

    R = 32

    def finish(b):
        def body(t, carry):
            at = pl.ds(pl.multiple_of(t * R, R), R)
            c = COLT[at, :]
            m0, r0, k0, m1, r1, k1 = (jnp.broadcast_to(c[:, j : j + 1], (R, 128)) for j in range(6))
            lab = jnp.broadcast_to(LABC[b, at, 0:1], (R, 128))
            lane = lax.broadcasted_iota(jnp.int32, (R, 128), 1).astype(F32)
            l0 = l1 = d0 = d1 = 0.0
            for k in range(SL // 128):
                ln = slice(k * 128, k * 128 + 128)
                x0 = X[0, b, at, ln] - m0
                x1 = X[1, b, at, ln] - m1
                e0 = jnp.exp2(x0 * HALF_LOG2E)
                e1 = jnp.exp2(x1 * HALF_LOG2E)
                s0 = e0 * r0
                s1 = e1 * r1
                q0 = s0.astype(BF16).astype(F32)
                q1 = s1.astype(BF16).astype(F32)
                hot = jnp.where(lane == lab - float(k * 128), 0.5, 0.0)
                G[0, at, ln] = (e0 * e0 * k0 - hot + (s0 - q1)).astype(BF16)
                G[1, at, ln] = (e1 * e1 * k1 - hot + (s1 - q0)).astype(BF16)
                l0 = l0 + (q1 + hot) * x0
                l1 = l1 + (q0 + hot) * x1
                d0 = d0 + (s0 - q0)
                d1 = d1 + (s1 - q1)
            l0 = l0 - m0 * d1
            l1 = l1 - m1 * d0
            LA[0, :, :] = LA[0] + fold_rows(l0)
            LA[1, :, :] = LA[1] + fold_rows(l1)
            return carry

        lax.fori_loop(0, GI // R, body, 0)

    def wgrad(i, b, start, count, rows, first):
        def body(t, carry):
            j = lax.rem(start + t, D // rows)
            at = pl.ds(pl.multiple_of(j * rows, rows), rows)
            d = jnp.dot(FT[i, b, at, :], G[i], preferred_element_type=F32)
            ACC[i, at, :] = d if first else ACC[i, at, :] + d
            return carry

        lax.fori_loop(0, count, body, 0)

    LA[...] = jnp.zeros_like(LA)
    LS[...] = jnp.zeros_like(LS)

    def wsend(kind, yy, half, o):
        push(WS.at[1, quarter(yy, half)], WS.at[1, quarter(yy, half)], ws.at[kind], wr.at[kind], ypeer(o))

    def wwait(kind, yy, half):
        arrive(WS.at[1, quarter(yy, half)], ws.at[kind], wr.at[kind])

    yd, yu, yo = lax.rem(y + NY - 1, NY), lax.rem(y + 1, NY), lax.rem(y + 2, NY)

    for c in loc:
        c.wait()
    fwait(0, 4, 0, xh, ok, 0, HALF)
    logits(0, 0, xh)
    wwait(0, y, 0)
    wsend(2, y, 0, 1)
    wwait(1, y, 1)
    wsend(4, y, 1, NY - 1)
    wsend(3, y, 1, 1)
    wsend(5, y, 0, NY - 1)
    pass_on(0)
    own_to_neighbours(1)
    transpose(0, 0, xh)
    fwait(1, 4, 0, xh, ok, 0, HALF)
    wwait(2, yd, 0)
    wsend(6, yd, 0, 1)
    wwait(4, yu, 1)
    wsend(7, yu, 1, NY - 1)
    logits(0, 1, xh)
    share_rest(0)
    transpose(0, 1, xh)
    for n, (_, bb, c) in enumerate(lab_kinds):
        arrive(LAB.at[flip(xh, bb), flip(core, c)], ls.at[n], lr.at[n])
    label_columns()
    wwait(3, yd, 1)
    wwait(5, yu, 0)
    wwait(6, yo, 0)
    wwait(7, yo, 1)
    shared_neighbours(0)
    logits(1, 0, 0)
    share_far(0)
    logits(1, 0, 1)
    shared_far(0)
    logits(0, 0, ox)
    send_stats(0)
    transpose(0, 0, ox)
    pass_on(1)
    transpose(1, 0, 0)
    transpose(1, 0, 1)
    wait_stats(0)
    combine(0)
    finish(0)
    share_rest(1)
    shared_neighbours(1)
    logits(1, 1, 0)
    logits(1, 1, 1)
    share_far(1)
    transpose(1, 1, 0)
    transpose(1, 1, 1)
    shared_far(1)
    logits(0, 1, ox)
    send_stats(1)
    transpose(0, 1, ox)
    wgrad(0, 0, 0, 1, D, True)
    wgrad(1, 0, 0, 1, D, True)
    wait_stats(1)
    combine(1)
    finish(1)

    def ring(n, me, H, chunk, S, RB, ssem, rsem, toward):
        steps = n // 2
        for t in range(steps):
            d = steps - t
            for way in range(2):
                j = lax.rem(me + (n - d if way == 0 else d), n)
                out = S[t]
                if t == 0:
                    out[way, :, :] = chunk(j, way * H, H).astype(out.dtype)
                else:
                    arrive(RB[t - 1].at[way], ssem.at[way, t - 1], rsem.at[way, t - 1])
                    if t == 1:
                        for half in range(2):
                            v = chunk(j, half * H, H)
                            if half == way:
                                v = v + RB[0][way].astype(F32)
                            out[way, half * H : half * H + H, :] = v.astype(out.dtype)
                    else:
                        v = chunk(j, 0, 2 * H) + RB[t - 1][way].astype(F32)
                        out[way, :, :] = v.astype(out.dtype)
                push(out.at[way], RB[t].at[way], ssem.at[way, t], rsem.at[way, t], toward[way])
            yield
        for way in range(2):
            arrive(RB[steps - 1].at[way], ssem.at[way, steps - 1], rsem.at[way, steps - 1])

    ydirs, zdirs = (ypeer(NY - 1), ypeer(1)), (zpeer(NZ - 1), zpeer(1))

    def acc_chunk(i, size):
        def chunk(j, lo, rows):
            return ACC[i, pl.ds(pl.multiple_of(j * size + lo, 16), rows), :]

        return chunk

    c0, c1 = D // NZ, D // NY
    r0 = ring(NZ, z, c0 // 2, acc_chunk(0, c0), S00, R00, s00s, s00r, zdirs)
    r1 = ring(NY, y, c1 // 2, acc_chunk(1, c1), S10, R10, s10s, s10r, ydirs)

    def own0():
        at = pl.ds(pl.multiple_of(z * c0, 16), c0)
        ACC[0, at, :] = ACC[0, at, :] + (R00[-1][0].astype(F32) + R00[-1][1].astype(F32))

    def own1():
        at = pl.ds(pl.multiple_of(y * c1, 16), c1)
        ACC[1, at, :] = ACC[1, at, :] + (R10[-1][0].astype(F32) + R10[-1][1].astype(F32))

    def sub_chunk(i, first):
        def chunk(j, lo, rows):
            return ACC[i, pl.ds(pl.multiple_of(first + j * 32 + lo, 16), rows), :]

        return chunk

    q0 = ring(NY, y, 16, sub_chunk(0, z * c0), S01, R01, s01s, s01r, ydirs)
    q1 = ring(NZ, z, 16, sub_chunk(1, y * c1), S11, R11, s11s, s11r, zdirs)

    def go(gen):
        for _ in gen:
            return

    wgrad(0, 1, z + NZ // 2, 1, c0, False)
    go(r0)
    wgrad(1, 1, y + NY // 2, 1, c1, False)
    go(r1)
    wgrad(0, 1, z + NZ // 2 + 1, NZ - 1, c0, False)
    go(r0)
    wgrad(1, 1, y + NY // 2 + 1, NY - 1, c1, False)
    go(r1)

    row = lax.broadcasted_iota(jnp.int32, (8, 128), 0)

    def put_rows(tile, r, v):
        tile = jnp.where(row == r, jnp.where(cp == 0, v[0], v[1]), tile)
        return jnp.where(row == 3 + r, jnp.where(cp == 0, v[1], v[0]), tile)

    lsums, wsums = [], []
    for i in range(2):
        wq = 0.0
        for h in range(2):
            at = pl.ds(pl.multiple_of(h * 512 + z * 64 + y * 16, 16), 16)
            wv = WS[i, at, :].astype(F32)
            wq = wq + fold_rows(fold_lanes(wv * wv))
        wsums.append(jnp.sum(wq, axis=0, keepdims=True))
        lsums.append(jnp.sum(LS[i] * 0.125 - LA[i], axis=0, keepdims=True))
    tile = put_rows(put_rows(jnp.zeros((8, 128), F32), 1, lsums), 2, wsums)

    go(r0)
    go(r0)
    go(r1)
    own1()
    go(q1)
    go(r0)
    own0()
    go(q0)
    go(q1)
    go(q0)
    go(q1)
    go(q0)
    go(q1)
    go(q1)

    inv = 1.0 / IMAGES
    sq = []
    for i in range(2):
        at = pl.ds(pl.multiple_of(z * c0 + y * 32 if i == 0 else y * c1 + z * 32, 32), 32)
        last = (R01 if i == 0 else R11)[-1]
        v = (ACC[i, at, :] + (last[0].astype(F32) + last[1].astype(F32))) * inv
        TB[i, :, :] = v
        sq.append(fold_rows(fold_lanes(v * v)))
    tile = put_rows(tile, 0, [jnp.sum(v, axis=0, keepdims=True) for v in sq])
    SCZ[0, :, :] = tile
    for o in range(1, NZ):
        push(SCZ.at[0], SCZ.at[o], zs.at[o - 1], zr.at[o - 1], zpeer(o))
    for n, g in enumerate(group):
        a, b, c = g
        off = pl.ds(pl.multiple_of((flip(xh, b) * 2 + flip(core, c)) * 8, 8), 8)
        push(TB.at[a, off], GB.at[:, my_s], as_.at[n], ar.at[n], peer(g))
    GB[:, my_s] = TB[0, pl.ds(pl.multiple_of((xh * 2 + core) * 8, 8), 8), :]
    for o in range(1, NZ):
        arrive(SCZ.at[o], zs.at[o - 1], zr.at[o - 1])
    SCY[0, :, :] = jnp.sum(SCZ[...], axis=0)
    for o in range(1, NY):
        push(SCY.at[0], SCY.at[o], ys.at[o - 1], yr.at[o - 1], ypeer(o))
    for o in range(1, NY):
        arrive(SCY.at[o], ys.at[o - 1], yr.at[o - 1])
    SCX[0, :, :] = jnp.sum(SCY[...], axis=0)
    for n, g in enumerate(group):
        push(SCX.at[0], SCX.at[slot(g)], xs.at[n], xr.at[n], peer(g))
    for n, g in enumerate(group):
        arrive(SCX.at[slot(g)], xs.at[n], xr.at[n])
    total = jnp.sum(SCX[...], axis=0)
    mine = jnp.where(cp == 0, total[0:3], total[3:6])
    mine = jnp.sum(mine, axis=1, keepdims=True)
    gnorm = jnp.sqrt(mine[0:1])
    wnorm = jnp.sqrt(mine[2:3])
    scale = trust * wnorm / (gnorm + decay * wnorm)
    loss_ref[...] = jnp.broadcast_to(mine[1:2] * inv, (8, 128))

    for n, (a, b, c) in enumerate(group):
        src = slice_of(flip(cp, a), flip(xh, b), flip(core, c))
        arrive(GB.at[:, src], as_.at[n], ar.at[n])
    w16 = W16[...].astype(F32)
    own_w = jnp.where(core == 0, w16[0:8], w16[8:16])
    out_ref[...] = scale * (GB[...] + decay * own_w)

    for c in sends:
        c.wait_send()


def on_device(features, labels, weight):
    lab = jnp.broadcast_to(labels.astype(F32)[None, :], (8, IMG))
    dma = pltpu.SemaphoreType.DMA
    vm = pltpu.VMEM
    any_ = pl.BlockSpec(memory_space=pl.ANY)
    ring_bufs = []
    ring_sems = []
    for rows, types in (
        (D // NZ, [BF16] * (NZ // 2 - 1) + [F32]),
        (32, [F32] * (NY // 2)),
        (D // NY, [BF16] * (NY // 2)),
        (32, [F32] * (NZ // 2)),
    ):
        bufs = tuple(vm((2, rows // 2 if t == 0 else rows, SL), dt) for t, dt in enumerate(types))
        ring_bufs += [bufs, bufs]
        ring_sems += [dma((2, len(types)))] * 2
    update, loss = pl.pallas_call(
        kernel,
        out_shape=(
            jax.ShapeDtypeStruct((8, CLASSES), F32),
            jax.ShapeDtypeStruct((8, 128), F32),
        ),
        in_specs=[any_, any_, any_],
        out_specs=(pl.BlockSpec(memory_space=vm), pl.BlockSpec(memory_space=vm)),
        scratch_shapes=[
            vm((2, 2, GI, D), BF16),
            vm((2, 2, D, GI), BF16),
            vm((2, D, SL), BF16),
            vm((16, CLASSES), BF16),
            vm((2, 2, 8, IMG), F32),
            vm((2, GI, 128), F32),
            vm((2, 2, GI, SL), F32),
            vm((2, GI, SL), BF16),
            vm((2, D, SL), F32),
            vm((8, 2, 8, GI), F32),
            vm((GI, 128), F32),
            vm((2, 8, 128), F32),
            vm((2, 8, 128), F32),
            vm((2, 32, SL), F32),
            vm((8, CLASSES), F32),
            vm((NZ, 8, 128), F32),
            vm((NY, 8, 128), F32),
            vm((8, 8, 128), F32),
            *ring_bufs,
            dma((5,)),
            dma((2, 13)), dma((2, 13)),
            dma((8,)), dma((8,)),
            dma((3,)), dma((3,)),
            dma((2, 7)), dma((2, 7)),
            dma((7,)), dma((7,)),
            dma((NZ - 1,)), dma((NZ - 1,)),
            dma((NY - 1,)), dma((NY - 1,)),
            dma((7,)), dma((7,)),
            *ring_sems,
        ],
        compiler_params=pltpu.CompilerParams(
            collective_id=0, has_side_effects=True, vmem_limit_bytes=56 * 2**20
        ),
    )(features[0], weight[0], lab)
    return (update[None], loss[0, :1])


def solution(mesh):
    placed = (P("copy", "dp", None), P("dp"), P("copy", None, None))
    return jax.shard_map(
        on_device,
        mesh=mesh,
        in_specs=placed,
        out_specs=(P("copy", "dp", None), P("copy")),
        check_vma=False,
    )
```
